256 devices in a mesh: pos: 64 (over x, z, core), pix: 4 (over y).
Axes of the slice: x: 4, y: 4, z: 8, core: 2. Of those that a mesh axis runs over, the one named last changes fastest.
Arguments:
- data: bfloat16 [65536, 16384], P('pos', 'pix'), may hold values from -64 to 64
- sketch_matrix: bfloat16 [16384, 256], P('pix'), may hold values from -0.046875 to 0.046875
Outputs:
- basis: float32 [65536, 256], P('pos')
- factor: float32 [256, 256], replicated
The draws below stay inside these ranges and needn't reach their ends.
All inputs are finite; a program needn't handle non-finite values.
Results may differ from the reference program's by a relative error of at most 0.0028.
Values may be sent and summed in bfloat16 or wider, within the bound.
A program may use at most 128 MiB of HBM per device.

```python
import math
import jax
import jax.numpy as jnp
from jax import lax

PIXELS = 16384
K = 256
POSITIONS = 65536


def draw_data(key, part):
    key = jax.random.fold_in(key, 11)
    key_base, key_rows, key_cols = jax.random.split(key, 3)
    base = jax.random.normal(key_base, (POSITIONS, PIXELS), jnp.float32)
    row_top = 10.0
    place = jnp.arange(POSITIONS, dtype=jnp.float32) / POSITIONS
    row_scale = jnp.exp(jax.random.uniform(key_rows, (POSITIONS, 1), jnp.float32) * math.log(row_top))
    row_scale = row_scale * jnp.exp(math.log(3.0) * place)[:, None]
    col_scale = jnp.exp(jax.random.uniform(key_cols, (1, PIXELS), jnp.float32) * math.log(10.0))
    return (base * row_scale * col_scale / 40.0).astype(jnp.bfloat16)


def level_of(rng, dims, shards, low, high):
    level = 1.0
    for axis_at, shards_of in shards:
        steps = jax.random.uniform(jax.random.fold_in(jax.random.fold_in(rng, 6), axis_at), (shards_of,), jnp.float32, low / len(shards), high / len(shards))
        level = level * jnp.repeat(jnp.exp(steps), dims[axis_at] // shards_of).reshape((-1,) + (1,) * (len(dims) - 1 - axis_at))
    return level


def scatter_about(own_key, extent, spread, bound, shards=(), kind=jnp.bfloat16):
    drawn = jax.random.normal(own_key, extent, jnp.float32) * spread
    if len(shards) > 0:
        drawn = level_of(own_key, extent, shards, -0.22, 0.18) * drawn
    return jnp.clip(drawn, min=-bound, max=bound).astype(kind)


def setup_inputs(seed: int = 0) -> dict:
    streams_of = jax.random.split(jax.random.key(seed), 3)
    return {
        "data": draw_data(jax.random.fold_in(streams_of[2], 71), 0),
        "sketch_matrix": scatter_about(streams_of[1], (PIXELS, K), PIXELS ** -0.5, 0.046875, ((0, 4),)),
    }


def orthonormal(sketch):
    gram = jnp.dot(sketch.T.astype(jnp.float32), sketch.astype(jnp.float32), precision=lax.Precision.HIGHEST, preferred_element_type=jnp.float32) / POSITIONS
    lower = jnp.linalg.cholesky(gram)
    basis = jax.scipy.linalg.solve_triangular(lower, sketch.T, lower=True).T
    return (basis, lower)

def reference(data, sketch_matrix):
    first = jnp.dot(data.astype(jnp.float32), sketch_matrix.astype(jnp.float32), preferred_element_type=jnp.float32)
    ortho, lower_one = orthonormal(first)
    ortho = ortho.astype(jnp.bfloat16)
    loads = lax.dot_general(data.astype(jnp.float32), ortho.astype(jnp.float32), (((0,), (0,)), ((), ())), preferred_element_type=jnp.float32)
    loads = (loads / POSITIONS).astype(jnp.bfloat16)
    second = jnp.dot(data.astype(jnp.float32), loads.astype(jnp.float32), preferred_element_type=jnp.float32)
    basis, lower_two = orthonormal(second)
    return (basis, lower_two.T)
```

```python
import functools

import jax
import jax.numpy as jnp
from jax import lax
from jax.experimental import pallas as pl
from jax.experimental.pallas import tpu as pltpu
from jax.sharding import PartitionSpec as P

MESH = pl.DeviceIdType.MESH
F32 = jnp.float32
BF16 = jnp.bfloat16
HIGHEST = lax.Precision.HIGHEST
K = 256
ROWS = 256
LANES = 128
PANEL = 64

NT = (((1,), (1,)), ((), ()))
TN = (((0,), (0,)), ((), ()))


def dims_of(mesh):
    pos, pix = mesh.shape["pos"], mesh.shape["pix"]
    if pos == 64:
        return 4, 8, 2, pix
    return 2, pos // 4, 2, pix


def factor_panel(square):
    n = square.shape[0]
    at_row = lax.broadcasted_iota(jnp.int32, (n, n), 0)
    at_col = lax.broadcasted_iota(jnp.int32, (n, n), 1)
    eye = jnp.where(at_row == at_col, 1.0, 0.0).astype(F32)
    state = jnp.concatenate([square, eye], axis=1)
    rows = lax.broadcasted_iota(jnp.int32, (n, 1), 0)
    scale = jnp.zeros((n, 1), F32)
    for j in range(n):
        row = state[j : j + 1, :]
        pivot = state[j : j + 1, j : j + 1]
        below = jnp.where(rows > j, state[:, j : j + 1], 0.0)
        scale = jnp.where(rows == j, pivot, scale)
        state = state - (below / pivot) * row
    state = state * lax.rsqrt(scale)
    upper = jnp.where(at_col >= at_row, state[:, :n], 0.0)
    return upper, state[:, n:]


def factorise(work, size=K):
    for b in range(size // PANEL):
        lo, hi = b * PANEL, (b + 1) * PANEL
        upper, inverse = factor_panel(work[lo:hi, lo:hi])
        top = jnp.dot(inverse, work[lo:hi, :], precision=HIGHEST, preferred_element_type=F32)
        at_row = lax.broadcasted_iota(jnp.int32, top.shape, 0) + lo
        at_col = lax.broadcasted_iota(jnp.int32, top.shape, 1)
        top = jnp.where(at_col >= at_row, top, 0.0)
        work[lo:hi, :] = top
        if hi < size:
            work[hi:, :] -= lax.dot_general(
                top[:, hi:size], top, TN, precision=HIGHEST, preferred_element_type=F32
            )


def identity_beside(work, gram, size=K):
    at_row = lax.broadcasted_iota(jnp.int32, (size, size), 0)
    at_col = lax.broadcasted_iota(jnp.int32, (size, size), 1)
    work[:, :size] = gram
    work[:, size:] = jnp.where(at_row == at_col, 1.0, 0.0).astype(F32)


def sketch_kernel(
    dims,
    total,
    data_hbm,
    sketch_hbm,
    second_out,
    gram_out,
    data,
    sketch,
    send_a,
    recv_a,
    own_a,
    first_t,
    recv_c,
    own_c,
    send_x,
    recv_x,
    send_z,
    recv_z,
    own_z,
    pair,
    loads,
    acc,
    recv_d,
    parts,
    gsum,
    gathered,
    zparts,
    work,
    load_sem,
    sem_a,
    sem_f,
    sem_c,
    sem_x,
    sem_z,
    sem_p,
    sem_lz,
    sem_lx,
    sem_lc,
    sem_d,
    sem_s,
    sem_g1,
    sem_g2,
    sem_g3,
):
    nx, nz, nc, ny = dims
    half = K // nc
    quarter = nz * LANES
    pos, y = lax.axis_index("pos"), lax.axis_index("pix")
    x, z, c = pos // (nz * nc), lax.rem(pos // nc, nz), lax.rem(pos, nc)
    group = nx * ny * nc
    mine = (x * ny + y) * nc + c
    share = K // group

    def at(px, pz, pc, py):
        return ((px * nz + pz) * nc + pc, py)

    def ahead(i, o, n):
        return lax.rem(i + o, n)

    def member(i):
        return at(i // (ny * nc), z, lax.rem(i, nc), lax.rem(i // nc, ny))

    def remote(src, dst, send_sem, recv_sem, device):
        return pltpu.make_async_remote_copy(
            src_ref=src,
            dst_ref=dst,
            send_sem=send_sem,
            recv_sem=recv_sem,
            device_id=device,
            device_id_type=MESH,
        )

    def rows_of(i):
        return pl.ds(pl.multiple_of(i * ROWS, ROWS), ROWS)

    y_order = list(range(1, ny)) + [0]
    x_order = list(range(1, nx)) + [0]

    sketch_load = pltpu.make_async_copy(sketch_hbm, sketch, load_sem.at[ny])
    sketch_load.start()
    data_loads = []
    for o in y_order:
        rows = rows_of(ahead(y, o, ny))
        load = pltpu.make_async_copy(data_hbm.at[rows], data.at[rows], load_sem.at[o])
        load.start()
        data_loads.append(load)

    barrier = pltpu.get_barrier_semaphore()

    def greet_group(o, carry):
        pl.semaphore_signal(
            barrier, inc=1, device_id=member(ahead(mine, o, group)), device_id_type=MESH
        )
        return carry

    def greet_z(o, carry):
        pl.semaphore_signal(
            barrier, inc=1, device_id=at(x, ahead(z, o, nz), c, y), device_id_type=MESH
        )
        return carry

    lax.fori_loop(1, group, greet_group, 0)
    lax.fori_loop(1, nz, greet_z, 0)
    sketch_load.wait()

    copies_a = []
    for i, o in enumerate(y_order):
        data_loads[i].wait()
        block = jnp.dot(
            data[rows_of(ahead(y, o, ny)), :], sketch[...], preferred_element_type=F32
        )
        if o == 0:
            own_a[...] = block
        else:
            send_a[o - 1] = block.astype(BF16)
            if i == 0:
                pl.semaphore_wait(barrier, group - 1 + nz - 1)
            copy = remote(
                send_a.at[o - 1],
                recv_a.at[o - 1],
                sem_a.at[0, o - 1],
                sem_a.at[1, o - 1],
                at(x, z, c, ahead(y, o, ny)),
            )
            copy.start()
            copies_a.append(copy)
    first = own_a[...]
    for i, copy in enumerate(copies_a):
        copy.wait_recv()
        first = first + recv_a[i].astype(F32)
    mine_t = first.astype(BF16).T
    first_t[y] = mine_t
    copies_f = []
    for o in range(1, ny):
        copy = remote(
            first_t.at[y],
            first_t.at[y],
            sem_f.at[0, o - 1],
            sem_f.at[1, o - 1],
            at(x, z, c, ahead(y, o, ny)),
        )
        copy.start()
        copies_f.append(copy)

    def gram_scatter(n):
        def step(o, carry):
            to = ahead(mine, o, group)
            remote(
                gsum.at[n, to],
                parts.at[n, o],
                sem_g1.at[n, 0, o],
                sem_g1.at[n, 1, o],
                member(to),
            ).start()
            return carry

        lax.fori_loop(1, group, step, 0)

    def gram_across(n):
        def step(o, sums):
            remote(
                gsum.at[n, mine],
                parts.at[n, o],
                sem_g1.at[n, 0, o],
                sem_g1.at[n, 1, o],
                member(ahead(mine, o, group)),
            ).wait()
            return sums + parts[n, o]

        sums = lax.fori_loop(1, group, step, gsum[n, mine])
        zparts[n, 0] = sums

        def send(o, carry):
            remote(
                zparts.at[n, 0],
                zparts.at[n, o],
                sem_g2.at[n, 0, o],
                sem_g2.at[n, 1, o],
                at(x, ahead(z, o, nz), c, y),
            ).start()
            return carry

        lax.fori_loop(1, nz, send, 0)

    def gram_gather(n):
        def step(o, carry):
            remote(
                zparts.at[n, 0],
                zparts.at[n, o],
                sem_g2.at[n, 0, o],
                sem_g2.at[n, 1, o],
                at(x, ahead(z, o, nz), c, y),
            ).wait()
            return carry

        lax.fori_loop(1, nz, step, 0)

        def add(plane, sums):
            return sums + zparts[n, lax.rem(z - plane + nz, nz)]

        sums = lax.fori_loop(0, nz, add, jnp.zeros((share, K), F32))
        gathered[n, mine] = sums * (1.0 / total)

        def send(o, carry):
            remote(
                gathered.at[n, mine],
                gathered.at[n, mine],
                sem_g3.at[n, 0, o],
                sem_g3.at[n, 1, o],
                member(ahead(mine, o, group)),
            ).start()
            return carry

        lax.fori_loop(1, group, send, 0)

    def gram_done(n):
        def step(o, carry):
            remote(
                gathered.at[n, mine],
                gathered.at[n, lax.rem(mine - o + group, group)],
                sem_g3.at[n, 0, o],
                sem_g3.at[n, 1, o],
                member(ahead(mine, o, group)),
            ).wait()
            return carry

        lax.fori_loop(1, group, step, 0)
        return gathered[n].reshape(K, K)

    gsum[0] = lax.dot_general(mine_t, mine_t, NT, preferred_element_type=F32).reshape(
        group, share, K
    )
    gram_scatter(0)
    for copy in copies_f:
        copy.wait_recv()

    copies_c, copies_x = [], []
    for i, o in enumerate(x_order):
        xd = ahead(x, o, nx)

        def tile(t, carry):
            cols = pl.ds(pl.multiple_of(xd * quarter + t * ROWS, ROWS), ROWS)
            here = pl.ds(pl.multiple_of(t * ROWS, ROWS), ROWS)
            block = jnp.zeros((K, ROWS), F32)
            for q in range(ny):
                block += jnp.dot(
                    first_t[q], data[q * ROWS : (q + 1) * ROWS, cols], preferred_element_type=F32
                )
            own_c[i, :, :, here] = block.reshape(nc, half, ROWS)
            return carry

        lax.fori_loop(0, quarter // ROWS, tile, 0)
        copy = remote(
            own_c.at[i, 1 - c],
            recv_c.at[i],
            sem_c.at[0, i],
            sem_c.at[1, i],
            at(x, z, 1 - c, y),
        )
        copy.start()
        copies_c.append(copy)
        if i == 0:
            gram_across(0)
        if i > 0:
            j = i - 1
            copies_c[j].wait_recv()
            send_x[j] = (own_c[j, c] + recv_c[j]).astype(BF16)
            copy = remote(
                send_x.at[j],
                recv_x.at[j],
                sem_x.at[0, j],
                sem_x.at[1, j],
                at(ahead(x, x_order[j], nx), z, c, y),
            )
            copy.start()
            copies_x.append(copy)
    gram_gather(0)

    identity_beside(work, gram_done(0))
    factorise(work)

    last = nx - 1
    copies_c[last].wait_recv()
    for copy in copies_x:
        copy.wait_recv()
    copies_z = []
    for o in list(range(1, nz)) + [0]:
        zd = ahead(z, o, nz)
        cols = pl.ds(pl.multiple_of(zd * LANES, LANES), LANES)
        block = own_c[last, c, :, cols] + recv_c[last, :, cols]
        for j in range(nx - 1):
            block = block + recv_x[j, :, cols].astype(F32)
        if o == 0:
            own_z[...] = block
        else:
            send_z[o - 1] = block.astype(BF16)
            copy = remote(
                send_z.at[o - 1],
                recv_z.at[o - 1],
                sem_z.at[0, o - 1],
                sem_z.at[1, o - 1],
                at(x, zd, c, y),
            )
            copy.start()
            copies_z.append(copy)
    block = own_z[...]
    for j, copy in enumerate(copies_z):
        copy.wait_recv()
        block = block + recv_z[j].astype(F32)
    pair[c] = block
    copy_p = remote(pair.at[c], pair.at[c], sem_p.at[0], sem_p.at[1], at(x, z, 1 - c, y))
    copy_p.start()
    copy_p.wait_recv()

    own_rows = pl.ds(pl.multiple_of(c * half, half), half)
    solved = jnp.dot(
        work[own_rows, K:],
        pair[...].reshape(K, LANES),
        precision=HIGHEST,
        preferred_element_type=F32,
    )

    def cell(px, pz, pc):
        cols = pl.ds(pl.multiple_of((px * nz + pz) * LANES, LANES), LANES)
        return loads.at[pl.ds(pl.multiple_of(pc * half, half), half), cols]

    cell(x, z, c)[...] = (solved * (1.0 / total)).astype(BF16)

    def over_z(o):
        return remote(
            cell(x, z, c),
            cell(x, z, c),
            sem_lz.at[0, o],
            sem_lz.at[1, o],
            at(x, ahead(z, o, nz), c, y),
        )

    def over_x(ox, oz):
        this = cell(x, lax.rem(z - oz + nz, nz), c)
        return remote(
            this, this, sem_lx.at[0, ox, oz], sem_lx.at[1, ox, oz], at(ahead(x, ox, nx), z, c, y)
        )

    def over_c(ox, oz):
        this = cell(lax.rem(x - ox + nx, nx), lax.rem(z - oz + nz, nz), c)
        return remote(
            this, this, sem_lc.at[0, ox, oz], sem_lc.at[1, ox, oz], at(x, z, 1 - c, y)
        )

    for o in range(1, nz):
        over_z(o).start()

    def forward(oz, carry):
        @pl.when(oz > 0)
        def _():
            over_z(oz).wait_recv()

        for ox in range(1, nx):
            over_x(ox, oz).start()
        over_c(0, oz).start()
        return carry

    lax.fori_loop(0, nz, forward, 0)

    for ox in range(nx):
        def pass_on(oz, carry):
            over_x(ox, oz).wait_recv()
            over_c(ox, oz).start()
            return carry

        def arrived(oz, carry):
            over_c(ox, oz).wait_recv()
            return carry

        if ox > 0:
            lax.fori_loop(0, nz, pass_on, 0)
        lax.fori_loop(0, nz, arrived, 0)
        cols = pl.ds(
            pl.multiple_of(lax.rem(x - ox + nx, nx) * quarter, quarter), quarter
        )
        copies_d = []
        for o in y_order:
            rows = rows_of(ahead(y, o, ny))
            term = lax.dot_general(data[rows, cols], loads[:, cols], NT, preferred_element_type=F32)
            if ox == 0:
                acc[o] = term
            else:
                acc[o] += term
            if ox == nx - 1 and o > 0:
                copy = remote(
                    acc.at[o],
                    recv_d.at[o - 1],
                    sem_d.at[0, o - 1],
                    sem_d.at[1, o - 1],
                    at(x, z, c, ahead(y, o, ny)),
                )
                copy.start()
                copies_d.append(copy)
    second = acc[0]
    for j, copy in enumerate(copies_d):
        copy.wait_recv()
        second = second + recv_d[j]
    second_out[y] = second

    gsum[1] = lax.dot_general(
        second, second, TN, precision=HIGHEST, preferred_element_type=F32
    ).reshape(group, share, K)
    gram_scatter(1)
    copies_s = []
    for o in range(1, ny):
        copy = remote(
            second_out.at[y],
            second_out.at[y],
            sem_s.at[0, o - 1],
            sem_s.at[1, o - 1],
            at(x, z, c, ahead(y, o, ny)),
        )
        copy.start()
        copies_s.append(copy)
    gram_across(1)
    gram_gather(1)
    gram_out[...] = gram_done(1)

    for copy in copies_s:
        copy.wait()
    for copy in copies_a + copies_f + copies_c + copies_x + copies_z + copies_d + [copy_p]:
        copy.wait_send()

    def drain(oz, carry):
        for ox in range(1, nx):
            over_x(ox, oz).wait_send()
        for ox in range(nx):
            over_c(ox, oz).wait_send()
        return carry

    def drain_z(oz, carry):
        over_z(oz).wait_send()
        return carry

    lax.fori_loop(0, nz, drain, 0)
    lax.fori_loop(1, nz, drain_z, 0)


def basis_kernel(second, gram, basis, factor, work):
    identity_beside(work, gram[...])
    factorise(work)
    factor[...] = work[:, :K]
    inverse = work[:, K:]
    for q in range(second.shape[0] // ROWS):
        rows = pl.ds(q * ROWS, ROWS)
        basis[rows, :] = lax.dot_general(
            second[rows, :], inverse, NT, precision=HIGHEST, preferred_element_type=F32
        )


def per_device(dims, data, sketch_matrix):
    nx, nz, nc, ny = dims
    rows, pixels = data.shape
    total = rows * nx * nz * nc
    half, quarter, group = K // nc, nz * LANES, nx * ny * nc
    share = K // group
    assert rows == ny * ROWS and pixels == nx * quarter
    vm = pltpu.VMEM
    dma = pltpu.SemaphoreType.DMA
    second, gram = pl.pallas_call(
        functools.partial(sketch_kernel, dims, total),
        out_shape=(
            jax.ShapeDtypeStruct((ny, ROWS, K), F32),
            jax.ShapeDtypeStruct((K, K), F32),
        ),
        in_specs=[pl.BlockSpec(memory_space=pl.ANY)] * 2,
        out_specs=(pl.BlockSpec(memory_space=pltpu.VMEM),) * 2,
        scratch_shapes=[
            vm((rows, pixels), BF16),
            vm((pixels, K), BF16),
            vm((ny - 1, ROWS, K), BF16),
            vm((ny - 1, ROWS, K), BF16),
            vm((ROWS, K), F32),
            vm((ny, K, ROWS), BF16),
            vm((nx, half, quarter), F32),
            vm((nx, nc, half, quarter), F32),
            vm((nx - 1, half, quarter), BF16),
            vm((nx - 1, half, quarter), BF16),
            vm((nz - 1, half, LANES), BF16),
            vm((nz - 1, half, LANES), BF16),
            vm((half, LANES), F32),
            vm((nc, half, LANES), F32),
            vm((K, pixels), BF16),
            vm((ny, ROWS, K), F32),
            vm((ny - 1, ROWS, K), F32),
            vm((2, group, share, K), F32),
            vm((2, group, share, K), F32),
            vm((2, group, share, K), F32),
            vm((2, nz, share, K), F32),
            vm((K, 2 * K), F32),
            dma((ny + 1,)),
            dma((2, ny - 1)),
            dma((2, ny - 1)),
            dma((2, nx)),
            dma((2, nx - 1)),
            dma((2, nz - 1)),
            dma((2,)),
            dma((2, nz)),
            dma((2, nx, nz)),
            dma((2, nx, nz)),
            dma((2, ny - 1)),
            dma((2, ny - 1)),
            dma((2, 2, group)),
            dma((2, 2, nz)),
            dma((2, 2, group)),
        ],
        compiler_params=pltpu.CompilerParams(
            collective_id=0, has_side_effects=True, vmem_limit_bytes=50 * 1024 * 1024
        ),
        cost_estimate=pl.CostEstimate(
            flops=6 * rows * pixels * K, bytes_accessed=2 * rows * pixels, transcendentals=0
        ),
        name="sketch",
    )(data, sketch_matrix)
    basis, factor = pl.pallas_call(
        basis_kernel,
        out_shape=(
            jax.ShapeDtypeStruct((rows, K), F32),
            jax.ShapeDtypeStruct((K, K), F32),
        ),
        in_specs=[pl.BlockSpec(memory_space=pltpu.VMEM)] * 2,
        out_specs=(pl.BlockSpec(memory_space=pltpu.VMEM),) * 2,
        scratch_shapes=[pltpu.VMEM((K, 2 * K), F32)],
        compiler_params=pltpu.CompilerParams(vmem_limit_bytes=32 * 1024 * 1024),
        name="basis",
    )(second.reshape(rows, K), gram)
    return basis, factor


def solution(mesh):
    in_specs = (P("pos", "pix"), P("pix", None))
    out_specs = (P("pos", None), P())
    return jax.shard_map(
        functools.partial(per_device, dims_of(mesh)),
        mesh=mesh,
        in_specs=in_specs,
        out_specs=out_specs,
        check_vma=False,
    )
```

```python
import functools

import jax
import jax.numpy as jnp
from jax import lax
from jax.experimental import pallas as pl
from jax.experimental.pallas import tpu as pltpu
from jax.sharding import PartitionSpec as P

MESH = pl.DeviceIdType.MESH
F32 = jnp.float32
BF16 = jnp.bfloat16
HIGHEST = lax.Precision.HIGHEST
K = 256
ROWS = 256
LANES = 128
PANEL = 64
SUB = 8

NT = (((1,), (1,)), ((), ()))
TN = (((0,), (0,)), ((), ()))


def dims_of(mesh):
    pos, pix = mesh.shape["pos"], mesh.shape["pix"]
    nx = 4 if pos >= 16 else 2
    return nx, pos // (2 * nx), 2, pix


def spread(column):
    return jnp.broadcast_to(column, (SUB, 2 * PANEL))


def factor_panel(square):
    n = square.shape[0]
    at_row = lax.broadcasted_iota(jnp.int32, (n, n), 0)
    at_col = lax.broadcasted_iota(jnp.int32, (n, n), 1)
    eye = jnp.where(at_row == at_col, 1.0, 0.0).astype(F32)
    state = jnp.concatenate([square, eye], axis=1)
    groups = n // SUB
    rows = [state[SUB * g : SUB * (g + 1), :] for g in range(groups)]
    sub = lax.broadcasted_iota(jnp.int32, (SUB, 2 * n), 0)
    lane = lax.broadcasted_iota(jnp.int32, (SUB, 2 * n), 1)
    done = []
    for g in range(groups):
        at = SUB * g
        cols = {
            h: [spread(rows[h][:, at + k : at + k + 1]) for k in range(SUB)]
            for h in range(g, groups)
        }
        top, panel = rows[g], cols[g]
        pivots = jnp.ones((SUB, 2 * n), F32)
        for j in range(SUB):
            pivot = panel[j][j : j + 1, :]
            inverse = 1.0 / pivot
            pivots = jnp.where(sub == j, pivot, pivots)
            heads = [panel[k][j : j + 1, :] for k in range(SUB)]
            row = top[j : j + 1, :]
            below = jnp.where(sub > j, panel[j], 0.0) * inverse
            for k in range(j + 1, SUB):
                panel[k] = panel[k] - below * heads[k]
            top = top - below * row
            for h in range(g + 1, groups):
                scaled = cols[h][j] * inverse
                for k in range(j + 1, SUB):
                    cols[h][k] = cols[h][k] - scaled * heads[k]
                rows[h] = rows[h] - scaled * row
        done.append(jnp.where(lane >= sub + at, top * lax.rsqrt(pivots), 0.0))
    state = jnp.concatenate(done, axis=0)
    return state[:, :n], state[:, n:]


def factorise(work, size=K):
    for b in range(size // PANEL):
        lo, hi = b * PANEL, (b + 1) * PANEL
        upper, inverse = factor_panel(work[lo:hi, lo:hi])
        top = jnp.dot(inverse, work[lo:hi, :], precision=HIGHEST, preferred_element_type=F32)
        at_row = lax.broadcasted_iota(jnp.int32, top.shape, 0) + lo
        at_col = lax.broadcasted_iota(jnp.int32, top.shape, 1)
        top = jnp.where(at_col >= at_row, top, 0.0)
        work[lo:hi, :] = top
        if hi < size:
            work[hi:, :] -= lax.dot_general(
                top[:, hi:size], top, TN, precision=HIGHEST, preferred_element_type=F32
            )


def identity_beside(work, gram, size=K):
    at_row = lax.broadcasted_iota(jnp.int32, (size, size), 0)
    at_col = lax.broadcasted_iota(jnp.int32, (size, size), 1)
    work[:, :size] = gram
    work[:, size:] = jnp.where(at_row == at_col, 1.0, 0.0).astype(F32)


def sketch_kernel(
    dims,
    total,
    data_hbm,
    sketch_hbm,
    basis_out,
    factor_out,
    data,
    sketch,
    send_a,
    recv_a,
    own_a,
    first_t,
    recv_c,
    own_c,
    send_x,
    recv_x,
    send_z,
    recv_z,
    own_z,
    pair,
    loads,
    acc,
    recv_d,
    send_far,
    recv_far,
    second,
    parts,
    gsum,
    gathered,
    zparts,
    work,
    load_sem,
    sem_a,
    sem_f,
    sem_c,
    sem_x,
    sem_z,
    sem_p,
    sem_lz,
    sem_lx,
    sem_lc,
    sem_d,
    sem_s,
    sem_g1,
    sem_g2,
    sem_g3,
):
    nx, nz, nc, ny = dims
    half = K // nc
    quarter = nz * LANES
    pos, y = lax.axis_index("pos"), lax.axis_index("pix")
    x, z, c = pos // (nz * nc), lax.rem(pos // nc, nz), lax.rem(pos, nc)
    group = nx * ny * nc
    mine = (x * ny + y) * nc + c
    share = K // group

    def at(px, pz, pc, py):
        return ((px * nz + pz) * nc + pc, py)

    def ahead(i, o, n):
        return lax.rem(i + o, n)

    def member(i):
        return at(i // (ny * nc), z, lax.rem(i, nc), lax.rem(i // nc, ny))

    def remote(src, dst, send_sem, recv_sem, device):
        return pltpu.make_async_remote_copy(
            src_ref=src,
            dst_ref=dst,
            send_sem=send_sem,
            recv_sem=recv_sem,
            device_id=device,
            device_id_type=MESH,
        )

    def rows_of(i):
        return pl.ds(pl.multiple_of(i * ROWS, ROWS), ROWS)

    def by_distance(n):
        return sorted(range(1, n), key=lambda o: (-min(o, n - o), o)) + [0]

    y_order, x_order, z_order = by_distance(ny), by_distance(nx), by_distance(nz)
    near_first = z_order[::-1]

    sketch_load = pltpu.make_async_copy(sketch_hbm, sketch, load_sem.at[ny])
    sketch_load.start()
    data_loads = []
    for o in y_order:
        rows = rows_of(ahead(y, o, ny))
        load = pltpu.make_async_copy(data_hbm.at[rows], data.at[rows], load_sem.at[o])
        load.start()
        data_loads.append(load)

    barrier = pltpu.get_barrier_semaphore()

    def greet_group(o, carry):
        pl.semaphore_signal(
            barrier, inc=1, device_id=member(ahead(mine, o, group)), device_id_type=MESH
        )
        return carry

    def greet_z(o, carry):
        pl.semaphore_signal(
            barrier, inc=1, device_id=at(x, ahead(z, o, nz), c, y), device_id_type=MESH
        )
        return carry

    lax.fori_loop(1, group, greet_group, 0)
    lax.fori_loop(1, nz, greet_z, 0)
    sketch_load.wait()

    copies_a = []
    for i, o in enumerate(y_order):
        data_loads[i].wait()
        block = jnp.dot(
            data[rows_of(ahead(y, o, ny)), :], sketch[...], preferred_element_type=F32
        )
        if o == 0:
            own_a[...] = block
        else:
            send_a[o - 1] = block.astype(BF16)
            if i == 0:
                pl.semaphore_wait(barrier, group - 1 + nz - 1)
            copy = remote(
                send_a.at[o - 1],
                recv_a.at[o - 1],
                sem_a.at[0, o - 1],
                sem_a.at[1, o - 1],
                at(x, z, c, ahead(y, o, ny)),
            )
            copy.start()
            copies_a.append(copy)
    first = own_a[...]
    for copy in copies_a:
        copy.wait_recv()
    for o in range(1, ny):
        first = first + recv_a[o - 1].astype(F32)
    mine_t = first.astype(BF16).T
    first_t[y] = mine_t
    copies_f = {}
    for o in y_order[:-1]:
        copy = remote(
            first_t.at[y],
            first_t.at[y],
            sem_f.at[0, o - 1],
            sem_f.at[1, o - 1],
            at(x, z, c, ahead(y, o, ny)),
        )
        copy.start()
        copies_f[o] = copy

    def gram_scatter(n):
        def step(o, carry):
            to = ahead(mine, o, group)
            remote(
                gsum.at[n, to],
                parts.at[n, o],
                sem_g1.at[n, 0, o],
                sem_g1.at[n, 1, o],
                member(to),
            ).start()
            return carry

        lax.fori_loop(1, group, step, 0)

    def gram_across(n):
        def step(o, sums):
            remote(
                gsum.at[n, mine],
                parts.at[n, o],
                sem_g1.at[n, 0, o],
                sem_g1.at[n, 1, o],
                member(ahead(mine, o, group)),
            ).wait()
            return sums + parts[n, o]

        sums = lax.fori_loop(1, group, step, gsum[n, mine])
        zparts[n, 0] = sums

        def send(o, carry):
            remote(
                zparts.at[n, 0],
                zparts.at[n, o],
                sem_g2.at[n, 0, o],
                sem_g2.at[n, 1, o],
                at(x, ahead(z, o, nz), c, y),
            ).start()
            return carry

        lax.fori_loop(1, nz, send, 0)

    def gram_gather(n):
        def step(o, carry):
            remote(
                zparts.at[n, 0],
                zparts.at[n, o],
                sem_g2.at[n, 0, o],
                sem_g2.at[n, 1, o],
                at(x, ahead(z, o, nz), c, y),
            ).wait()
            return carry

        lax.fori_loop(1, nz, step, 0)

        def add(plane, sums):
            return sums + zparts[n, lax.rem(z - plane + nz, nz)]

        sums = lax.fori_loop(0, nz, add, jnp.zeros((share, K), F32))
        gathered[n, mine] = sums * (1.0 / total)

        def send(o, carry):
            remote(
                gathered.at[n, mine],
                gathered.at[n, mine],
                sem_g3.at[n, 0, o],
                sem_g3.at[n, 1, o],
                member(ahead(mine, o, group)),
            ).start()
            return carry

        lax.fori_loop(1, group, send, 0)

    def gram_done(n):
        def step(o, carry):
            remote(
                gathered.at[n, mine],
                gathered.at[n, lax.rem(mine - o + group, group)],
                sem_g3.at[n, 0, o],
                sem_g3.at[n, 1, o],
                member(ahead(mine, o, group)),
            ).wait()
            return carry

        lax.fori_loop(1, group, step, 0)
        return gathered[n].reshape(K, K)

    gsum[0] = lax.dot_general(mine_t, mine_t, NT, preferred_element_type=F32).reshape(
        group, share, K
    )
    gram_scatter(0)

    def add_rows(o, i):
        block_at = lax.rem(y - o + ny, ny)
        xd = ahead(x, x_order[i], nx)

        def tile(t, carry):
            cols = pl.ds(pl.multiple_of(xd * quarter + t * ROWS, ROWS), ROWS)
            here = pl.ds(pl.multiple_of(t * ROWS, ROWS), ROWS)
            block = jnp.dot(
                first_t[block_at], data[rows_of(block_at), cols], preferred_element_type=F32
            ).reshape(nc, half, ROWS)
            if o == 0:
                own_c[i, :, :, here] = block
            else:
                own_c[i, :, :, here] += block
            return carry

        lax.fori_loop(0, quarter // ROWS, tile, 0)

    arrivals = y_order[::-1]
    for o in arrivals[:-1]:
        if o > 0:
            copies_f[o].wait_recv()
        for i in range(nx):
            add_rows(o, i)
    copies_f[arrivals[-1]].wait_recv()
    copies_c, copies_x = [], []
    for i in range(nx):
        add_rows(arrivals[-1], i)
        copy = remote(
            own_c.at[i, 1 - c],
            recv_c.at[i],
            sem_c.at[0, i],
            sem_c.at[1, i],
            at(x, z, 1 - c, y),
        )
        copy.start()
        copies_c.append(copy)
    gram_across(0)
    for i in range(nx - 1):
        copies_c[i].wait_recv()
        send_x[i] = (own_c[i, c] + recv_c[i]).astype(BF16)
        copy = remote(
            send_x.at[i],
            recv_x.at[i],
            sem_x.at[0, i],
            sem_x.at[1, i],
            at(ahead(x, x_order[i], nx), z, c, y),
        )
        copy.start()
        copies_x.append(copy)
    gram_gather(0)
    last = nx - 1
    copies_c[last].wait_recv()
    for copy in copies_x:
        copy.wait_recv()
    copies_z = []
    for o in z_order:
        zd = ahead(z, o, nz)
        cols = pl.ds(pl.multiple_of(zd * LANES, LANES), LANES)
        block = own_c[last, c, :, cols] + recv_c[last, :, cols]
        for j in range(nx - 1):
            block = block + recv_x[j, :, cols].astype(F32)
        if o == 0:
            own_z[...] = block
        else:
            send_z[o - 1] = block.astype(BF16)
            copy = remote(
                send_z.at[o - 1],
                recv_z.at[o - 1],
                sem_z.at[0, o - 1],
                sem_z.at[1, o - 1],
                at(x, zd, c, y),
            )
            copy.start()
            copies_z.append(copy)

    identity_beside(work, gram_done(0))
    factorise(work)

    block = own_z[...]
    for copy in copies_z:
        copy.wait_recv()
    for j in range(nz - 1):
        block = block + recv_z[j].astype(F32)
    pair[c] = block
    copy_p = remote(pair.at[c], pair.at[c], sem_p.at[0], sem_p.at[1], at(x, z, 1 - c, y))
    copy_p.start()
    copy_p.wait_recv()

    own_rows = pl.ds(pl.multiple_of(c * half, half), half)
    solved = jnp.dot(
        work[own_rows, K:],
        pair[...].reshape(K, LANES),
        precision=HIGHEST,
        preferred_element_type=F32,
    )

    def cell(px, pz, pc):
        cols = pl.ds(pl.multiple_of((px * nz + pz) * LANES, LANES), LANES)
        return loads.at[pl.ds(pl.multiple_of(pc * half, half), half), cols]

    cell(x, z, c)[...] = (solved * (1.0 / total)).astype(BF16)

    def over_z(o):
        return remote(
            cell(x, z, c),
            cell(x, z, c),
            sem_lz.at[0, o],
            sem_lz.at[1, o],
            at(x, ahead(z, o, nz), c, y),
        )

    def over_x(ox, oz, hops):
        this = cell(lax.rem(x - ox + hops + nx, nx), lax.rem(z - oz + nz, nz), c)
        return remote(
            this,
            this,
            sem_lx.at[0, ox, oz],
            sem_lx.at[1, ox, oz],
            at(lax.rem(x + hops + nx, nx), z, c, y),
        )

    def over_c(ox, oz):
        this = cell(lax.rem(x - ox + nx, nx), lax.rem(z - oz + nz, nz), c)
        return remote(
            this, this, sem_lc.at[0, ox, oz], sem_lc.at[1, ox, oz], at(x, z, 1 - c, y)
        )

    for o in z_order[:-1]:
        over_z(o).start()
    steps = list(near_first)
    copies_lx = []

    def start_x(ox, oz, hops):
        copy = over_x(ox, oz, hops)
        copy.start()
        copies_lx.append(copy)

    for n in range(nz + 2):
        if n < nz:
            oz = steps[n]
            if oz > 0:
                over_z(oz).wait_recv()
            start_x(1, oz, 1)
            if nx > 2:
                start_x(nx - 1, oz, -1)
            over_c(0, oz).start()
        if n >= 2:
            oz = steps[n - 2]
            over_x(1, oz, 1).wait_recv()
            if nx == 4 and n % 2 == 0:
                start_x(2, oz, 1)
            over_c(1, oz).start()
            if nx == 4:
                over_x(3, oz, -1).wait_recv()
                if n % 2 == 1:
                    start_x(2, oz, -1)
                over_c(3, oz).start()

    def add_pixels(ox):
        for oz in steps:
            over_c(ox, oz).wait_recv()
        cols = pl.ds(
            pl.multiple_of(lax.rem(x - ox + nx, nx) * quarter, quarter), quarter
        )
        copies = []
        for o in y_order:
            rows = rows_of(ahead(y, o, ny))
            term = lax.dot_general(data[rows, cols], loads[:, cols], NT, preferred_element_type=F32)
            if ox > 0:
                term = acc[o] + term
            if ox != nx // 2 or 2 * o != ny:
                acc[o] = term
            if ox == nx // 2 and o > 0:
                if 2 * o == ny:
                    send_far[...] = term.astype(BF16)
                copy = remote(
                    send_far if 2 * o == ny else acc.at[o],
                    recv_far if 2 * o == ny else recv_d.at[o - 1],
                    sem_d.at[0, o - 1],
                    sem_d.at[1, o - 1],
                    at(x, z, c, ahead(y, o, ny)),
                )
                copy.start()
                copies.append(copy)
        return copies

    add_pixels(0)
    if nx == 4:
        for n, oz in enumerate(steps):
            over_x(2, oz, 1 if n % 2 == 0 else -1).wait_recv()
            over_c(2, oz).start()
        add_pixels(1)
        add_pixels(3)
    copies_d = add_pixels(nx // 2)
    mine_s = acc[0]
    for copy in copies_d:
        copy.wait_recv()
    for o in range(1, ny):
        mine_s = mine_s + (recv_far[...].astype(F32) if 2 * o == ny else recv_d[o - 1])
    second[y] = mine_s

    gsum[1] = lax.dot_general(
        mine_s, mine_s, TN, precision=HIGHEST, preferred_element_type=F32
    ).reshape(group, share, K)
    gram_scatter(1)
    gram_across(1)
    gram_gather(1)
    copies_s = []
    for o in y_order[:-1]:
        copy = remote(
            second.at[y],
            second.at[y],
            sem_s.at[0, o - 1],
            sem_s.at[1, o - 1],
            at(x, z, c, ahead(y, o, ny)),
        )
        copy.start()
        copies_s.append(copy)
    identity_beside(work, gram_done(1))
    factorise(work)
    factor_out[...] = work[:, :K]
    for copy in copies_s:
        copy.wait()
    for q in range(ny):
        basis_out[q * ROWS : (q + 1) * ROWS, :] = lax.dot_general(
            second[q], work[:, K:], NT, precision=HIGHEST, preferred_element_type=F32
        )

    copies = copies_a + list(copies_f.values()) + copies_c + copies_x + copies_z + copies_d
    for copy in copies + copies_lx + [copy_p]:
        copy.wait_send()
    for oz in range(nz):
        if oz > 0:
            over_z(oz).wait_send()
        for ox in range(nx):
            over_c(ox, oz).wait_send()


def per_device(dims, data, sketch_matrix):
    nx, nz, nc, ny = dims
    rows, pixels = data.shape
    total = rows * nx * nz * nc
    half, quarter, group = K // nc, nz * LANES, nx * ny * nc
    share = K // group
    assert rows == ny * ROWS and pixels == nx * quarter
    vm = pltpu.VMEM
    dma = pltpu.SemaphoreType.DMA
    return pl.pallas_call(
        functools.partial(sketch_kernel, dims, total),
        out_shape=(
            jax.ShapeDtypeStruct((rows, K), F32),
            jax.ShapeDtypeStruct((K, K), F32),
        ),
        in_specs=[pl.BlockSpec(memory_space=pl.ANY)] * 2,
        out_specs=(pl.BlockSpec(memory_space=pltpu.VMEM),) * 2,
        scratch_shapes=[
            vm((rows, pixels), BF16),
            vm((pixels, K), BF16),
            vm((ny - 1, ROWS, K), BF16),
            vm((ny - 1, ROWS, K), BF16),
            vm((ROWS, K), F32),
            vm((ny, K, ROWS), BF16),
            vm((nx, half, quarter), F32),
            vm((nx, nc, half, quarter), F32),
            vm((nx - 1, half, quarter), BF16),
            vm((nx - 1, half, quarter), BF16),
            vm((nz - 1, half, LANES), BF16),
            vm((nz - 1, half, LANES), BF16),
            vm((half, LANES), F32),
            vm((nc, half, LANES), F32),
            vm((K, pixels), BF16),
            vm((ny, ROWS, K), F32),
            vm((ny - 1, ROWS, K), F32),
            vm((ROWS, K), BF16),
            vm((ROWS, K), BF16),
            vm((ny, ROWS, K), F32),
            vm((2, group, share, K), F32),
            vm((2, group, share, K), F32),
            vm((2, group, share, K), F32),
            vm((2, nz, share, K), F32),
            vm((K, 2 * K), F32),
            dma((ny + 1,)),
            dma((2, ny - 1)),
            dma((2, ny - 1)),
            dma((2, nx)),
            dma((2, nx - 1)),
            dma((2, nz - 1)),
            dma((2,)),
            dma((2, nz)),
            dma((2, nx, nz)),
            dma((2, nx, nz)),
            dma((2, ny - 1)),
            dma((2, ny - 1)),
            dma((2, 2, group)),
            dma((2, 2, nz)),
            dma((2, 2, group)),
        ],
        compiler_params=pltpu.CompilerParams(
            collective_id=0, has_side_effects=True, vmem_limit_bytes=60 * 1024 * 1024
        ),
        cost_estimate=pl.CostEstimate(
            flops=6 * rows * pixels * K, bytes_accessed=2 * rows * pixels, transcendentals=0
        ),
        name="sketch",
    )(data, sketch_matrix)


def solution(mesh):
    in_specs = (P("pos", "pix"), P("pix", None))
    out_specs = (P("pos", None), P())
    return jax.shard_map(
        functools.partial(per_device, dims_of(mesh)),
        mesh=mesh,
        in_specs=in_specs,
        out_specs=out_specs,
        check_vma=False,
    )
```

```python
import functools

import jax
import jax.numpy as jnp
from jax import lax
from jax.experimental import pallas as pl
from jax.experimental.pallas import tpu as pltpu
from jax.sharding import PartitionSpec as P

MESH = pl.DeviceIdType.MESH
F32 = jnp.float32
BF16 = jnp.bfloat16
HIGHEST = lax.Precision.HIGHEST
K = 256
ROWS = 256
LANES = 128
PANEL = 64
PANELS = range(K // PANEL)
SUB = 8

NT = (((1,), (1,)), ((), ()))
TN = (((0,), (0,)), ((), ()))


def dims_of(mesh):
    pos, pix = mesh.shape["pos"], mesh.shape["pix"]
    nx = 4 if pos >= 16 else 2
    return nx, pos // (2 * nx), 2, pix


def spread(column):
    return jnp.broadcast_to(column, (SUB, 2 * PANEL))


def factor_panel(square):
    n = square.shape[0]
    at_row = lax.broadcasted_iota(jnp.int32, (n, n), 0)
    at_col = lax.broadcasted_iota(jnp.int32, (n, n), 1)
    eye = jnp.where(at_row == at_col, 1.0, 0.0).astype(F32)
    state = jnp.concatenate([square, eye], axis=1)
    groups = n // SUB
    rows = [state[SUB * g : SUB * (g + 1), :] for g in range(groups)]
    sub = lax.broadcasted_iota(jnp.int32, (SUB, 2 * n), 0)
    lane = lax.broadcasted_iota(jnp.int32, (SUB, 2 * n), 1)
    done = []
    for g in range(groups):
        at = SUB * g
        cols = {
            h: [spread(rows[h][:, at + k : at + k + 1]) for k in range(SUB)]
            for h in range(g, groups)
        }
        top, panel = rows[g], cols[g]
        pivots = jnp.ones((SUB, 2 * n), F32)
        for j in range(SUB):
            pivot = panel[j][j : j + 1, :]
            inverse = 1.0 / pivot
            pivots = jnp.where(sub == j, pivot, pivots)
            heads = [panel[k][j : j + 1, :] for k in range(SUB)]
            row = top[j : j + 1, :]
            below = jnp.where(sub > j, panel[j], 0.0) * inverse
            for k in range(j + 1, SUB):
                panel[k] = panel[k] - below * heads[k]
            top = top - below * row
            for h in range(g + 1, groups):
                scaled = cols[h][j] * inverse
                for k in range(j + 1, SUB):
                    cols[h][k] = cols[h][k] - scaled * heads[k]
                rows[h] = rows[h] - scaled * row
        done.append(jnp.where(lane >= sub + at, top * lax.rsqrt(pivots), 0.0))
    state = jnp.concatenate(done, axis=0)
    return state[:, :n], state[:, n:]


def factorise(work, panels, size=K):
    for b in panels:
        lo, hi = b * PANEL, (b + 1) * PANEL
        upper, inverse = factor_panel(work[lo:hi, lo:hi])
        top = jnp.dot(inverse, work[lo:hi, :], precision=HIGHEST, preferred_element_type=F32)
        at_row = lax.broadcasted_iota(jnp.int32, top.shape, 0) + lo
        at_col = lax.broadcasted_iota(jnp.int32, top.shape, 1)
        top = jnp.where(at_col >= at_row, top, 0.0)
        work[lo:hi, :] = top
        if hi < size:
            work[hi:, :] -= lax.dot_general(
                top[:, hi:size], top, TN, precision=HIGHEST, preferred_element_type=F32
            )


def identity_beside(work, gram, size=K):
    at_row = lax.broadcasted_iota(jnp.int32, (size, size), 0)
    at_col = lax.broadcasted_iota(jnp.int32, (size, size), 1)
    work[:, :size] = gram
    work[:, size:] = jnp.where(at_row == at_col, 1.0, 0.0).astype(F32)


def sketch_kernel(
    dims,
    total,
    data_hbm,
    sketch_hbm,
    second_out,
    work_out,
    data,
    sketch,
    send_a,
    recv_a,
    own_a,
    first_t,
    recv_c,
    own_c,
    send_x,
    recv_x,
    send_z,
    recv_z,
    own_z,
    pair,
    loads,
    acc,
    recv_d,
    send_far,
    recv_far,
    parts,
    gsum,
    gathered,
    zparts,
    work,
    load_sem,
    sem_a,
    sem_f,
    sem_c,
    sem_x,
    sem_z,
    sem_p,
    sem_lz,
    sem_lx,
    sem_lc,
    sem_d,
    sem_s,
    sem_g,
):
    nx, nz, nc, ny = dims
    half = K // nc
    quarter = nz * LANES
    pos, y = lax.axis_index("pos"), lax.axis_index("pix")
    x, z, c = pos // (nz * nc), lax.rem(pos // nc, nz), lax.rem(pos, nc)
    group = nx * ny * nc
    mine = (x * ny + y) * nc + c
    share = K // group

    def at(px, pz, pc, py):
        return ((px * nz + pz) * nc + pc, py)

    def ahead(i, o, n):
        return lax.rem(i + o, n)

    def member(i):
        return at(i // (ny * nc), z, lax.rem(i, nc), lax.rem(i // nc, ny))

    def remote(src, dst, send_sem, recv_sem, device):
        return pltpu.make_async_remote_copy(
            src_ref=src,
            dst_ref=dst,
            send_sem=send_sem,
            recv_sem=recv_sem,
            device_id=device,
            device_id_type=MESH,
        )

    def rows_of(i):
        return pl.ds(pl.multiple_of(i * ROWS, ROWS), ROWS)

    def by_distance(n):
        return sorted(range(1, n), key=lambda o: (-min(o, n - o), o)) + [0]

    y_order, x_order, z_order = by_distance(ny), by_distance(nx), by_distance(nz)
    near_first = z_order[::-1]

    sketch_load = pltpu.make_async_copy(sketch_hbm, sketch, load_sem.at[ny])
    sketch_load.start()
    data_loads = []
    for o in y_order:
        rows = rows_of(ahead(y, o, ny))
        load = pltpu.make_async_copy(data_hbm.at[rows], data.at[rows], load_sem.at[o])
        load.start()
        data_loads.append(load)

    barrier = pltpu.get_barrier_semaphore()

    def greet_group(o, carry):
        pl.semaphore_signal(
            barrier, inc=1, device_id=member(ahead(mine, o, group)), device_id_type=MESH
        )
        return carry

    def greet_z(o, carry):
        pl.semaphore_signal(
            barrier, inc=1, device_id=at(x, ahead(z, o, nz), c, y), device_id_type=MESH
        )
        return carry

    lax.fori_loop(1, group, greet_group, 0)
    lax.fori_loop(1, nz, greet_z, 0)
    sketch_load.wait()

    copies_a = []
    for i, o in enumerate(y_order):
        data_loads[i].wait()
        block = jnp.dot(
            data[rows_of(ahead(y, o, ny)), :], sketch[...], preferred_element_type=F32
        )
        if o == 0:
            own_a[...] = block
        else:
            send_a[o - 1] = block.astype(BF16)
            if i == 0:
                pl.semaphore_wait(barrier, group - 1 + nz - 1)
            copy = remote(
                send_a.at[o - 1],
                recv_a.at[o - 1],
                sem_a.at[0, o - 1],
                sem_a.at[1, o - 1],
                at(x, z, c, ahead(y, o, ny)),
            )
            copy.start()
            copies_a.append(copy)
    first = own_a[...]
    for copy in copies_a:
        copy.wait_recv()
    for o in range(1, ny):
        first = first + recv_a[o - 1].astype(F32)
    mine_t = first.astype(BF16).T
    first_t[y] = mine_t
    copies_f = {}
    for o in y_order[:-1]:
        copy = remote(
            first_t.at[y],
            first_t.at[y],
            sem_f.at[0, o - 1],
            sem_f.at[1, o - 1],
            at(x, z, c, ahead(y, o, ny)),
        )
        copy.start()
        copies_f[o] = copy

    def wait_all(ref, sem):
        pltpu.make_async_copy(ref, ref, sem).wait()

    def gram_scatter(n):
        def step(o, carry):
            to = ahead(mine, o, group)
            remote(
                gsum.at[n, to],
                parts.at[n, o - 1],
                sem_g.at[n, 0, 0],
                sem_g.at[n, 0, 1],
                member(to),
            ).start()
            return carry

        lax.fori_loop(1, group, step, 0)

    def gram_across(n):
        others = parts.at[n, 0 : group - 1]
        wait_all(others, sem_g.at[n, 0, 1])
        zparts[n, 0] = gsum[n, mine] + jnp.sum(others[...], axis=0)

        def send(o, carry):
            remote(
                zparts.at[n, 0],
                zparts.at[n, o],
                sem_g.at[n, 1, 0],
                sem_g.at[n, 1, 1],
                at(x, ahead(z, o, nz), c, y),
            ).start()
            return carry

        lax.fori_loop(1, nz, send, 0)

    def gram_gather(n):
        wait_all(zparts.at[n, 1:nz], sem_g.at[n, 1, 1])

        def add(plane, sums):
            return sums + zparts[n, lax.rem(z - plane + nz, nz)]

        sums = lax.fori_loop(0, nz, add, jnp.zeros((share, K), F32))
        gathered[n, mine] = sums * (1.0 / total)

        def send(o, carry):
            remote(
                gathered.at[n, mine],
                gathered.at[n, mine],
                sem_g.at[n, 2, 0],
                sem_g.at[n, 2, 1],
                member(ahead(mine, o, group)),
            ).start()
            return carry

        lax.fori_loop(1, group, send, 0)

    def gram_done(n):
        wait_all(gathered.at[n, 0 : group - 1], sem_g.at[n, 2, 1])
        return gathered[n].reshape(K, K)

    def gram_sent(n):
        wait_all(parts.at[n, 0 : group - 1], sem_g.at[n, 0, 0])
        wait_all(zparts.at[n, 1:nz], sem_g.at[n, 1, 0])
        wait_all(gathered.at[n, 0 : group - 1], sem_g.at[n, 2, 0])

    gsum[0] = lax.dot_general(mine_t, mine_t, NT, preferred_element_type=F32).reshape(
        group, share, K
    )
    gram_scatter(0)

    def add_rows(o, i):
        block_at = lax.rem(y - o + ny, ny)
        xd = ahead(x, x_order[i], nx)

        def tile(t, carry):
            cols = pl.ds(pl.multiple_of(xd * quarter + t * ROWS, ROWS), ROWS)
            here = pl.ds(pl.multiple_of(t * ROWS, ROWS), ROWS)
            block = jnp.dot(
                first_t[block_at], data[rows_of(block_at), cols], preferred_element_type=F32
            ).reshape(nc, half, ROWS)
            if o == 0:
                own_c[i, :, :, here] = block
            else:
                own_c[i, :, :, here] += block
            return carry

        lax.fori_loop(0, quarter // ROWS, tile, 0)

    arrivals = y_order[::-1]
    for o in arrivals[:-1]:
        if o > 0:
            copies_f[o].wait_recv()
        for i in range(nx):
            add_rows(o, i)
    gram_across(0)
    copies_f[arrivals[-1]].wait_recv()
    copies_c, copies_x = [], []
    for i in range(nx):
        add_rows(arrivals[-1], i)
        copy = remote(
            own_c.at[i, 1 - c],
            recv_c.at[i],
            sem_c.at[0, i],
            sem_c.at[1, i],
            at(x, z, 1 - c, y),
        )
        copy.start()
        copies_c.append(copy)
    for i in range(nx - 1):
        copies_c[i].wait_recv()
        send_x[i] = (own_c[i, c] + recv_c[i]).astype(BF16)
        copy = remote(
            send_x.at[i],
            recv_x.at[i],
            sem_x.at[0, i],
            sem_x.at[1, i],
            at(ahead(x, x_order[i], nx), z, c, y),
        )
        copy.start()
        copies_x.append(copy)
    gram_gather(0)

    identity_beside(work, gram_done(0))
    factorise(work, PANELS[:-1])

    last = nx - 1
    copies_c[last].wait_recv()
    for copy in copies_x:
        copy.wait_recv()
    copies_z = []
    for o in z_order:
        zd = ahead(z, o, nz)
        cols = pl.ds(pl.multiple_of(zd * LANES, LANES), LANES)
        block = own_c[last, c, :, cols] + recv_c[last, :, cols]
        for j in range(nx - 1):
            block = block + recv_x[j, :, cols].astype(F32)
        if o == 0:
            own_z[...] = block
        else:
            send_z[o - 1] = block.astype(BF16)
            copy = remote(
                send_z.at[o - 1],
                recv_z.at[o - 1],
                sem_z.at[0, o - 1],
                sem_z.at[1, o - 1],
                at(x, zd, c, y),
            )
            copy.start()
            copies_z.append(copy)
    factorise(work, PANELS[-1:])
    block = own_z[...]
    for copy in copies_z:
        copy.wait_recv()
    for j in range(nz - 1):
        block = block + recv_z[j].astype(F32)
    pair[c] = block
    copy_p = remote(pair.at[c], pair.at[c], sem_p.at[0], sem_p.at[1], at(x, z, 1 - c, y))
    copy_p.start()
    copy_p.wait_recv()

    own_rows = pl.ds(pl.multiple_of(c * half, half), half)
    solved = jnp.dot(
        work[own_rows, K:],
        pair[...].reshape(K, LANES),
        precision=HIGHEST,
        preferred_element_type=F32,
    )

    def cell(px, pz, pc):
        cols = pl.ds(pl.multiple_of((px * nz + pz) * LANES, LANES), LANES)
        return loads.at[pl.ds(pl.multiple_of(pc * half, half), half), cols]

    cell(x, z, c)[...] = (solved * (1.0 / total)).astype(BF16)

    def over_z(o):
        return remote(
            cell(x, z, c),
            cell(x, z, c),
            sem_lz.at[0, o],
            sem_lz.at[1, o],
            at(x, ahead(z, o, nz), c, y),
        )

    def over_x(ox, oz, hops):
        this = cell(lax.rem(x - ox + hops + nx, nx), lax.rem(z - oz + nz, nz), c)
        return remote(
            this,
            this,
            sem_lx.at[0, ox, oz],
            sem_lx.at[1, ox, oz],
            at(lax.rem(x + hops + nx, nx), z, c, y),
        )

    def over_c(ox):
        cols = pl.ds(pl.multiple_of(lax.rem(x - ox + nx, nx) * quarter, quarter), quarter)
        this = loads.at[own_rows, cols]
        return remote(this, this, sem_lc.at[0, ox], sem_lc.at[1, ox], at(x, z, 1 - c, y))

    for o in z_order[:-1]:
        over_z(o).start()
    steps = list(near_first)
    copies_lx = []

    def start_x(ox, oz, hops):
        copy = over_x(ox, oz, hops)
        copy.start()
        copies_lx.append(copy)

    for n in range(nz + 2):
        if n < nz:
            oz = steps[n]
            if oz > 0:
                over_z(oz).wait_recv()
            start_x(1, oz, 1)
            if nx > 2:
                start_x(nx - 1, oz, -1)
            if n == nz - 1:
                over_c(0).start()
        if n >= 2:
            oz = steps[n - 2]
            over_x(1, oz, 1).wait_recv()
            if nx == 4 and n % 2 == 0:
                start_x(2, oz, 1)
            if nx == 4:
                over_x(3, oz, -1).wait_recv()
                if n % 2 == 1:
                    start_x(2, oz, -1)

    over_c(1).start()
    if nx == 4:
        over_c(3).start()

    def add_pixels(ox):
        over_c(ox).wait_recv()
        cols = pl.ds(
            pl.multiple_of(lax.rem(x - ox + nx, nx) * quarter, quarter), quarter
        )
        copies = []
        for o in y_order:
            rows = rows_of(ahead(y, o, ny))
            term = lax.dot_general(data[rows, cols], loads[:, cols], NT, preferred_element_type=F32)
            if ox > 0:
                term = acc[o] + term
            if ox != nx // 2 or 2 * o != ny:
                acc[o] = term
            if ox == nx // 2 and o > 0:
                if 2 * o == ny:
                    send_far[...] = term.astype(BF16)
                copy = remote(
                    send_far if 2 * o == ny else acc.at[o],
                    recv_far if 2 * o == ny else recv_d.at[o - 1],
                    sem_d.at[0, o - 1],
                    sem_d.at[1, o - 1],
                    at(x, z, c, ahead(y, o, ny)),
                )
                copy.start()
                copies.append(copy)
        return copies

    add_pixels(0)
    if nx == 4:
        for n, oz in enumerate(steps):
            over_x(2, oz, 1 if n % 2 == 0 else -1).wait_recv()
        over_c(2).start()
        add_pixels(1)
        add_pixels(3)
    copies_d = add_pixels(nx // 2)
    mine_s = acc[0]
    for copy in copies_d:
        copy.wait_recv()
    for o in range(1, ny):
        mine_s = mine_s + (recv_far[...].astype(F32) if 2 * o == ny else recv_d[o - 1])
    second_out[y] = mine_s

    gsum[1] = lax.dot_general(
        mine_s, mine_s, TN, precision=HIGHEST, preferred_element_type=F32
    ).reshape(group, share, K)
    gram_scatter(1)
    gram_across(1)
    gram_gather(1)
    copies_s = []
    for o in y_order[:-1]:
        copy = remote(
            second_out.at[y],
            second_out.at[y],
            sem_s.at[0, o - 1],
            sem_s.at[1, o - 1],
            at(x, z, c, ahead(y, o, ny)),
        )
        copy.start()
        copies_s.append(copy)

    copies = copies_a + list(copies_f.values()) + copies_c + copies_x + copies_z + copies_d
    for copy in copies + copies_lx + [copy_p]:
        copy.wait_send()
    for oz in range(1, nz):
        over_z(oz).wait_send()
    for ox in range(nx):
        over_c(ox).wait_send()
    gram_sent(0)

    identity_beside(work_out, gram_done(1))
    factorise(work_out, PANELS)
    gram_sent(1)
    for copy in copies_s:
        copy.wait()


def basis_kernel(second, work, basis, factor):
    basis[...] = lax.dot_general(
        second[0], work[:, K:], NT, precision=HIGHEST, preferred_element_type=F32
    )
    factor[...] = work[:, :K]


def per_device(dims, data, sketch_matrix):
    nx, nz, nc, ny = dims
    rows, pixels = data.shape
    total = rows * nx * nz * nc
    half, quarter, group = K // nc, nz * LANES, nx * ny * nc
    share = K // group
    assert rows == ny * ROWS and pixels == nx * quarter
    vm = pltpu.VMEM
    dma = pltpu.SemaphoreType.DMA
    second, work = pl.pallas_call(
        functools.partial(sketch_kernel, dims, total),
        out_shape=(
            jax.ShapeDtypeStruct((ny, ROWS, K), F32),
            jax.ShapeDtypeStruct((K, 2 * K), F32),
        ),
        in_specs=[pl.BlockSpec(memory_space=pl.ANY)] * 2,
        out_specs=(pl.BlockSpec(memory_space=pltpu.VMEM),) * 2,
        scratch_shapes=[
            vm((rows, pixels), BF16),
            vm((pixels, K), BF16),
            vm((ny - 1, ROWS, K), BF16),
            vm((ny - 1, ROWS, K), BF16),
            vm((ROWS, K), F32),
            vm((ny, K, ROWS), BF16),
            vm((nx, half, quarter), F32),
            vm((nx, nc, half, quarter), F32),
            vm((nx - 1, half, quarter), BF16),
            vm((nx - 1, half, quarter), BF16),
            vm((nz - 1, half, LANES), BF16),
            vm((nz - 1, half, LANES), BF16),
            vm((half, LANES), F32),
            vm((nc, half, LANES), F32),
            vm((K, pixels), BF16),
            vm((ny, ROWS, K), F32),
            vm((ny - 1, ROWS, K), F32),
            vm((ROWS, K), BF16),
            vm((ROWS, K), BF16),
            vm((2, group, share, K), F32),
            vm((2, group, share, K), F32),
            vm((2, group, share, K), F32),
            vm((2, nz, share, K), F32),
            vm((K, 2 * K), F32),
            dma((ny + 1,)),
            dma((2, ny - 1)),
            dma((2, ny - 1)),
            dma((2, nx)),
            dma((2, nx - 1)),
            dma((2, nz - 1)),
            dma((2,)),
            dma((2, nz)),
            dma((2, nx, nz)),
            dma((2, nx)),
            dma((2, ny - 1)),
            dma((2, ny - 1)),
            dma((2, 3, 2)),
        ],
        compiler_params=pltpu.CompilerParams(
            collective_id=0, has_side_effects=True, vmem_limit_bytes=60 * 1024 * 1024
        ),
        cost_estimate=pl.CostEstimate(
            flops=6 * rows * pixels * K, bytes_accessed=2 * rows * pixels, transcendentals=0
        ),
        name="sketch",
    )(data, sketch_matrix)
    return pl.pallas_call(
        basis_kernel,
        grid=(ny,),
        out_shape=(
            jax.ShapeDtypeStruct((rows, K), F32),
            jax.ShapeDtypeStruct((K, K), F32),
        ),
        in_specs=[
            pl.BlockSpec((1, ROWS, K), lambda q: (q, 0, 0)),
            pl.BlockSpec((K, 2 * K), lambda q: (0, 0)),
        ],
        out_specs=(
            pl.BlockSpec((ROWS, K), lambda q: (q, 0)),
            pl.BlockSpec((K, K), lambda q: (0, 0)),
        ),
        compiler_params=pltpu.CompilerParams(vmem_limit_bytes=60 * 1024 * 1024),
        name="basis",
    )(second, work)


def solution(mesh):
    in_specs = (P("pos", "pix"), P("pix", None))
    out_specs = (P("pos", None), P())
    return jax.shard_map(
        functools.partial(per_device, dims_of(mesh)),
        mesh=mesh,
        in_specs=in_specs,
        out_specs=out_specs,
        check_vma=False,
    )
```

```python
import functools

import jax
import jax.numpy as jnp
from jax import lax
from jax.experimental import pallas as pl
from jax.experimental.pallas import tpu as pltpu
from jax.sharding import PartitionSpec as P

MESH = pl.DeviceIdType.MESH
F32 = jnp.float32
BF16 = jnp.bfloat16
HIGHEST = lax.Precision.HIGHEST
K = 256
ROWS = 256
LANES = 128
PANEL = 64
PANELS = range(K // PANEL)
SUB = 8

NT = (((1,), (1,)), ((), ()))
TN = (((0,), (0,)), ((), ()))


def dims_of(mesh):
    pos, pix = mesh.shape["pos"], mesh.shape["pix"]
    nx = 4 if pos >= 16 else 2
    return nx, pos // (2 * nx), 2, pix


def spread(column):
    return jnp.broadcast_to(column, (SUB, 2 * PANEL))


def factor_panel(square):
    n = square.shape[0]
    at_row = lax.broadcasted_iota(jnp.int32, (n, n), 0)
    at_col = lax.broadcasted_iota(jnp.int32, (n, n), 1)
    eye = jnp.where(at_row == at_col, 1.0, 0.0).astype(F32)
    state = jnp.concatenate([square, eye], axis=1)
    groups = n // SUB
    rows = [state[SUB * g : SUB * (g + 1), :] for g in range(groups)]
    sub = lax.broadcasted_iota(jnp.int32, (SUB, 2 * n), 0)
    lane = lax.broadcasted_iota(jnp.int32, (SUB, 2 * n), 1)
    done = []
    for g in range(groups):
        at = SUB * g
        cols = {
            h: [spread(rows[h][:, at + k : at + k + 1]) for k in range(SUB)]
            for h in range(g, groups)
        }
        top, panel = rows[g], cols[g]
        pivots = jnp.ones((SUB, 2 * n), F32)
        for j in range(SUB):
            pivot = panel[j][j : j + 1, :]
            inverse = 1.0 / pivot
            pivots = jnp.where(sub == j, pivot, pivots)
            heads = [panel[k][j : j + 1, :] for k in range(SUB)]
            row = top[j : j + 1, :]
            below = jnp.where(sub > j, panel[j], 0.0) * inverse
            for k in range(j + 1, SUB):
                panel[k] = panel[k] - below * heads[k]
            top = top - below * row
            for h in range(g + 1, groups):
                scaled = cols[h][j] * inverse
                for k in range(j + 1, SUB):
                    cols[h][k] = cols[h][k] - scaled * heads[k]
                rows[h] = rows[h] - scaled * row
        done.append(jnp.where(lane >= sub + at, top * lax.rsqrt(pivots), 0.0))
    state = jnp.concatenate(done, axis=0)
    return state[:, :n], state[:, n:]


def factorise(work, panels, size=K):
    for b in panels:
        lo, hi = b * PANEL, (b + 1) * PANEL
        upper, inverse = factor_panel(work[lo:hi, lo:hi])
        top = jnp.dot(inverse, work[lo:hi, :], precision=HIGHEST, preferred_element_type=F32)
        at_row = lax.broadcasted_iota(jnp.int32, top.shape, 0) + lo
        at_col = lax.broadcasted_iota(jnp.int32, top.shape, 1)
        top = jnp.where(at_col >= at_row, top, 0.0)
        work[lo:hi, :] = top
        if hi < size:
            work[hi:, :] -= lax.dot_general(
                top[:, hi:size], top, TN, precision=HIGHEST, preferred_element_type=F32
            )


def identity_beside(work, gram, size=K):
    at_row = lax.broadcasted_iota(jnp.int32, (size, size), 0)
    at_col = lax.broadcasted_iota(jnp.int32, (size, size), 1)
    work[:, :size] = gram
    work[:, size:] = jnp.where(at_row == at_col, 1.0, 0.0).astype(F32)


def sketch_kernel(
    dims,
    total,
    data_hbm,
    sketch_hbm,
    second_out,
    work_out,
    data,
    sketch,
    send_a,
    recv_a,
    own_a,
    first_t,
    recv_c,
    own_c,
    send_x,
    recv_x,
    send_z,
    recv_z,
    own_z,
    pair,
    loads,
    acc,
    recv_d,
    send_far,
    recv_far,
    parts,
    gsum,
    gathered,
    zparts,
    work,
    load_sem,
    sem_a,
    sem_f,
    sem_c,
    sem_x,
    sem_z,
    sem_p,
    sem_lz,
    sem_lx,
    sem_lc,
    sem_d,
    sem_s,
    sem_g,
):
    nx, nz, nc, ny = dims
    half = K // nc
    quarter = nz * LANES
    pos, y = lax.axis_index("pos"), lax.axis_index("pix")
    x, z, c = pos // (nz * nc), lax.rem(pos // nc, nz), lax.rem(pos, nc)
    group = nx * ny * nc
    mine = (x * ny + y) * nc + c
    share = K // group

    def at(px, pz, pc, py):
        return ((px * nz + pz) * nc + pc, py)

    def ahead(i, o, n):
        return lax.rem(i + o, n)

    def member(i):
        return at(i // (ny * nc), z, lax.rem(i, nc), lax.rem(i // nc, ny))

    def remote(src, dst, send_sem, recv_sem, device):
        return pltpu.make_async_remote_copy(
            src_ref=src,
            dst_ref=dst,
            send_sem=send_sem,
            recv_sem=recv_sem,
            device_id=device,
            device_id_type=MESH,
        )

    def rows_of(i):
        return pl.ds(pl.multiple_of(i * ROWS, ROWS), ROWS)

    def by_distance(n):
        return sorted(range(1, n), key=lambda o: (-min(o, n - o), o)) + [0]

    y_order, x_order, z_order = by_distance(ny), by_distance(nx), by_distance(nz)
    near_first = z_order[::-1]

    sketch_load = pltpu.make_async_copy(sketch_hbm, sketch, load_sem.at[ny])
    sketch_load.start()
    data_loads = []
    for o in y_order:
        rows = rows_of(ahead(y, o, ny))
        load = pltpu.make_async_copy(data_hbm.at[rows], data.at[rows], load_sem.at[o])
        load.start()
        data_loads.append(load)

    barrier = pltpu.get_barrier_semaphore()

    def greet_group(o, carry):
        pl.semaphore_signal(
            barrier, inc=1, device_id=member(ahead(mine, o, group)), device_id_type=MESH
        )
        return carry

    def greet_z(o, carry):
        pl.semaphore_signal(
            barrier, inc=1, device_id=at(x, ahead(z, o, nz), c, y), device_id_type=MESH
        )
        return carry

    lax.fori_loop(1, group, greet_group, 0)
    lax.fori_loop(1, nz, greet_z, 0)
    sketch_load.wait()

    copies_a = []
    for i, o in enumerate(y_order):
        data_loads[i].wait()
        block = jnp.dot(
            data[rows_of(ahead(y, o, ny)), :], sketch[...], preferred_element_type=F32
        )
        if o == 0:
            own_a[...] = block
        else:
            send_a[o - 1] = block.astype(BF16)
            if i == 0:
                pl.semaphore_wait(barrier, group - 1 + nz - 1)
            copy = remote(
                send_a.at[o - 1],
                recv_a.at[o - 1],
                sem_a.at[0, o - 1],
                sem_a.at[1, o - 1],
                at(x, z, c, ahead(y, o, ny)),
            )
            copy.start()
            copies_a.append(copy)
    first = own_a[...]
    for copy in copies_a:
        copy.wait_recv()
    for o in range(1, ny):
        first = first + recv_a[o - 1].astype(F32)
    mine_t = first.astype(BF16).T
    first_t[y] = mine_t
    copies_f = {}
    for o in y_order[:-1]:
        copy = remote(
            first_t.at[y],
            first_t.at[y],
            sem_f.at[0, o - 1],
            sem_f.at[1, o - 1],
            at(x, z, c, ahead(y, o, ny)),
        )
        copy.start()
        copies_f[o] = copy

    def wait_all(ref, sem):
        pltpu.make_async_copy(ref, ref, sem).wait()

    def gram_scatter(n):
        def step(o, carry):
            to = ahead(mine, o, group)
            remote(
                gsum.at[n, to],
                parts.at[n, o - 1],
                sem_g.at[n, 0, 0],
                sem_g.at[n, 0, 1],
                member(to),
            ).start()
            return carry

        lax.fori_loop(1, group, step, 0)

    def gram_across(n):
        others = parts.at[n, 0 : group - 1]
        wait_all(others, sem_g.at[n, 0, 1])
        zparts[n, 0] = gsum[n, mine] + jnp.sum(others[...], axis=0)

        def send(o, carry):
            remote(
                zparts.at[n, 0],
                zparts.at[n, o],
                sem_g.at[n, 1, 0],
                sem_g.at[n, 1, 1],
                at(x, ahead(z, o, nz), c, y),
            ).start()
            return carry

        lax.fori_loop(1, nz, send, 0)

    def gram_gather(n):
        wait_all(zparts.at[n, 1:nz], sem_g.at[n, 1, 1])

        def add(plane, sums):
            return sums + zparts[n, lax.rem(z - plane + nz, nz)]

        sums = lax.fori_loop(0, nz, add, jnp.zeros((share, K), F32))
        gathered[n, mine] = sums * (1.0 / total)

        def send(o, carry):
            remote(
                gathered.at[n, mine],
                gathered.at[n, mine],
                sem_g.at[n, 2, 0],
                sem_g.at[n, 2, 1],
                member(ahead(mine, o, group)),
            ).start()
            return carry

        lax.fori_loop(1, group, send, 0)

    def gram_done(n):
        wait_all(gathered.at[n, 0 : group - 1], sem_g.at[n, 2, 1])
        return gathered[n].reshape(K, K)

    def gram_sent(n):
        wait_all(parts.at[n, 0 : group - 1], sem_g.at[n, 0, 0])
        wait_all(zparts.at[n, 1:nz], sem_g.at[n, 1, 0])
        wait_all(gathered.at[n, 0 : group - 1], sem_g.at[n, 2, 0])

    gsum[0] = lax.dot_general(mine_t, mine_t, NT, preferred_element_type=F32).reshape(
        group, share, K
    )
    gram_scatter(0)

    def add_rows(offsets, i):
        xd = ahead(x, x_order[i], nx)

        def tile(t, carry):
            cols = pl.ds(pl.multiple_of(xd * quarter + t * ROWS, ROWS), ROWS)
            here = pl.ds(pl.multiple_of(t * ROWS, ROWS), ROWS)
            block = jnp.zeros((K, ROWS), F32)
            for o in offsets:
                block_at = lax.rem(y - o + ny, ny)
                block += jnp.dot(
                    first_t[block_at], data[rows_of(block_at), cols], preferred_element_type=F32
                )
            block = block.reshape(nc, half, ROWS)
            if 0 in offsets:
                own_c[i, :, :, here] = block
            else:
                own_c[i, :, :, here] += block
            return carry

        lax.fori_loop(0, quarter // ROWS, tile, 0)

    for i in range(nx):
        add_rows([0], i)
    for copy in copies_f.values():
        copy.wait_recv()
    gram_across(0)
    copies_c, copies_x = [], []
    for i in range(nx):
        add_rows(range(1, ny), i)
        copy = remote(
            own_c.at[i, 1 - c],
            recv_c.at[i],
            sem_c.at[0, i],
            sem_c.at[1, i],
            at(x, z, 1 - c, y),
        )
        copy.start()
        copies_c.append(copy)
        if i > 0:
            j = i - 1
            copies_c[j].wait_recv()
            send_x[j] = (own_c[j, c] + recv_c[j]).astype(BF16)
            copy = remote(
                send_x.at[j],
                recv_x.at[j],
                sem_x.at[0, j],
                sem_x.at[1, j],
                at(ahead(x, x_order[j], nx), z, c, y),
            )
            copy.start()
            copies_x.append(copy)
    gram_gather(0)

    identity_beside(work, gram_done(0))
    factorise(work, PANELS[:2])

    last = nx - 1
    copies_c[last].wait_recv()
    for copy in copies_x:
        copy.wait_recv()
    copies_z = []
    for o in z_order:
        zd = ahead(z, o, nz)
        cols = pl.ds(pl.multiple_of(zd * LANES, LANES), LANES)
        block = own_c[last, c, :, cols] + recv_c[last, :, cols]
        for j in range(nx - 1):
            block = block + recv_x[j, :, cols].astype(F32)
        if o == 0:
            own_z[...] = block
        else:
            send_z[o - 1] = block.astype(BF16)
            copy = remote(
                send_z.at[o - 1],
                recv_z.at[o - 1],
                sem_z.at[0, o - 1],
                sem_z.at[1, o - 1],
                at(x, zd, c, y),
            )
            copy.start()
            copies_z.append(copy)
    factorise(work, PANELS[2:])
    block = own_z[...]
    for copy in copies_z:
        copy.wait_recv()
    for j in range(nz - 1):
        block = block + recv_z[j].astype(F32)
    pair[c] = block
    copy_p = remote(pair.at[c], pair.at[c], sem_p.at[0], sem_p.at[1], at(x, z, 1 - c, y))
    copy_p.start()
    copy_p.wait_recv()

    own_rows = pl.ds(pl.multiple_of(c * half, half), half)
    solved = jnp.dot(
        work[own_rows, K:],
        pair[...].reshape(K, LANES),
        precision=HIGHEST,
        preferred_element_type=F32,
    )

    def cell(px, pz, pc):
        cols = pl.ds(pl.multiple_of((px * nz + pz) * LANES, LANES), LANES)
        return loads.at[pl.ds(pl.multiple_of(pc * half, half), half), cols]

    cell(x, z, c)[...] = (solved * (1.0 / total)).astype(BF16)

    def over_z(o):
        return remote(
            cell(x, z, c),
            cell(x, z, c),
            sem_lz.at[0, o],
            sem_lz.at[1, o],
            at(x, ahead(z, o, nz), c, y),
        )

    def over_x(ox, oz, hops):
        this = cell(lax.rem(x - ox + hops + nx, nx), lax.rem(z - oz + nz, nz), c)
        return remote(
            this,
            this,
            sem_lx.at[0, ox, oz],
            sem_lx.at[1, ox, oz],
            at(lax.rem(x + hops + nx, nx), z, c, y),
        )

    def over_c(ox):
        cols = pl.ds(pl.multiple_of(lax.rem(x - ox + nx, nx) * quarter, quarter), quarter)
        this = loads.at[own_rows, cols]
        return remote(this, this, sem_lc.at[0, ox], sem_lc.at[1, ox], at(x, z, 1 - c, y))

    for o in z_order[:-1]:
        over_z(o).start()
    steps = list(near_first)
    copies_lx = []

    def start_x(ox, oz, hops):
        copy = over_x(ox, oz, hops)
        copy.start()
        copies_lx.append(copy)

    for n in range(nz + 2):
        if n < nz:
            oz = steps[n]
            if oz > 0:
                over_z(oz).wait_recv()
            start_x(1, oz, 1)
            if nx > 2:
                start_x(nx - 1, oz, -1)
            if n == nz - 1:
                over_c(0).start()
        if n >= 2:
            oz = steps[n - 2]
            over_x(1, oz, 1).wait_recv()
            if nx == 4 and n % 2 == 0:
                start_x(2, oz, 1)
            if nx == 4:
                over_x(3, oz, -1).wait_recv()
                if n % 2 == 1:
                    start_x(2, oz, -1)

    over_c(1).start()
    if nx == 4:
        over_c(3).start()

    def add_pixels(ox):
        over_c(ox).wait_recv()
        cols = pl.ds(
            pl.multiple_of(lax.rem(x - ox + nx, nx) * quarter, quarter), quarter
        )
        copies = []
        for o in y_order:
            rows = rows_of(ahead(y, o, ny))
            term = lax.dot_general(data[rows, cols], loads[:, cols], NT, preferred_element_type=F32)
            if ox > 0:
                term = acc[o] + term
            if ox != nx // 2 or 2 * o != ny:
                acc[o] = term
            if ox == nx // 2 and o > 0:
                if 2 * o == ny:
                    send_far[...] = term.astype(BF16)
                copy = remote(
                    send_far if 2 * o == ny else acc.at[o],
                    recv_far if 2 * o == ny else recv_d.at[o - 1],
                    sem_d.at[0, o - 1],
                    sem_d.at[1, o - 1],
                    at(x, z, c, ahead(y, o, ny)),
                )
                copy.start()
                copies.append(copy)
        return copies

    add_pixels(0)
    if nx == 4:
        for n, oz in enumerate(steps):
            over_x(2, oz, 1 if n % 2 == 0 else -1).wait_recv()
        over_c(2).start()
        add_pixels(1)
        add_pixels(3)
    copies_d = add_pixels(nx // 2)
    mine_s = acc[0]
    for copy in copies_d:
        copy.wait_recv()
    for o in range(1, ny):
        mine_s = mine_s + (recv_far[...].astype(F32) if 2 * o == ny else recv_d[o - 1])
    second_out[y] = mine_s

    gsum[1] = lax.dot_general(
        mine_s, mine_s, TN, precision=HIGHEST, preferred_element_type=F32
    ).reshape(group, share, K)
    gram_scatter(1)
    gram_across(1)
    gram_gather(1)
    copies_s = []
    for o in y_order[:-1]:
        copy = remote(
            second_out.at[y],
            second_out.at[y],
            sem_s.at[0, o - 1],
            sem_s.at[1, o - 1],
            at(x, z, c, ahead(y, o, ny)),
        )
        copy.start()
        copies_s.append(copy)

    copies = copies_a + list(copies_f.values()) + copies_c + copies_x + copies_z + copies_d
    for copy in copies + copies_lx + [copy_p]:
        copy.wait_send()
    for oz in range(1, nz):
        over_z(oz).wait_send()
    for ox in range(nx):
        over_c(ox).wait_send()
    gram_sent(0)

    identity_beside(work_out, gram_done(1))
    factorise(work_out, PANELS)
    gram_sent(1)
    for copy in copies_s:
        copy.wait()


def basis_kernel(second, work, basis, factor):
    basis[...] = lax.dot_general(
        second[0], work[:, K:], NT, precision=HIGHEST, preferred_element_type=F32
    )
    factor[...] = work[:, :K]


def per_device(dims, data, sketch_matrix):
    nx, nz, nc, ny = dims
    rows, pixels = data.shape
    total = rows * nx * nz * nc
    half, quarter, group = K // nc, nz * LANES, nx * ny * nc
    share = K // group
    assert rows == ny * ROWS and pixels == nx * quarter
    vm = pltpu.VMEM
    dma = pltpu.SemaphoreType.DMA
    second, work = pl.pallas_call(
        functools.partial(sketch_kernel, dims, total),
        out_shape=(
            jax.ShapeDtypeStruct((ny, ROWS, K), F32),
            jax.ShapeDtypeStruct((K, 2 * K), F32),
        ),
        in_specs=[pl.BlockSpec(memory_space=pl.ANY)] * 2,
        out_specs=(pl.BlockSpec(memory_space=pltpu.VMEM),) * 2,
        scratch_shapes=[
            vm((rows, pixels), BF16),
            vm((pixels, K), BF16),
            vm((ny - 1, ROWS, K), BF16),
            vm((ny - 1, ROWS, K), BF16),
            vm((ROWS, K), F32),
            vm((ny, K, ROWS), BF16),
            vm((nx, half, quarter), F32),
            vm((nx, nc, half, quarter), F32),
            vm((nx - 1, half, quarter), BF16),
            vm((nx - 1, half, quarter), BF16),
            vm((nz - 1, half, LANES), BF16),
            vm((nz - 1, half, LANES), BF16),
            vm((half, LANES), F32),
            vm((nc, half, LANES), F32),
            vm((K, pixels), BF16),
            vm((ny, ROWS, K), F32),
            vm((ny - 1, ROWS, K), F32),
            vm((ROWS, K), BF16),
            vm((ROWS, K), BF16),
            vm((2, group, share, K), F32),
            vm((2, group, share, K), F32),
            vm((2, group, share, K), F32),
            vm((2, nz, share, K), F32),
            vm((K, 2 * K), F32),
            dma((ny + 1,)),
            dma((2, ny - 1)),
            dma((2, ny - 1)),
            dma((2, nx)),
            dma((2, nx - 1)),
            dma((2, nz - 1)),
            dma((2,)),
            dma((2, nz)),
            dma((2, nx, nz)),
            dma((2, nx)),
            dma((2, ny - 1)),
            dma((2, ny - 1)),
            dma((2, 3, 2)),
        ],
        compiler_params=pltpu.CompilerParams(
            collective_id=0, has_side_effects=True, vmem_limit_bytes=60 * 1024 * 1024
        ),
        cost_estimate=pl.CostEstimate(
            flops=6 * rows * pixels * K, bytes_accessed=2 * rows * pixels, transcendentals=0
        ),
        name="sketch",
    )(data, sketch_matrix)
    return pl.pallas_call(
        basis_kernel,
        grid=(ny,),
        out_shape=(
            jax.ShapeDtypeStruct((rows, K), F32),
            jax.ShapeDtypeStruct((K, K), F32),
        ),
        in_specs=[
            pl.BlockSpec((1, ROWS, K), lambda q: (q, 0, 0)),
            pl.BlockSpec((K, 2 * K), lambda q: (0, 0)),
        ],
        out_specs=(
            pl.BlockSpec((ROWS, K), lambda q: (q, 0)),
            pl.BlockSpec((K, K), lambda q: (0, 0)),
        ),
        compiler_params=pltpu.CompilerParams(vmem_limit_bytes=60 * 1024 * 1024),
        name="basis",
    )(second, work)


def solution(mesh):
    in_specs = (P("pos", "pix"), P("pix", None))
    out_specs = (P("pos", None), P())
    return jax.shard_map(
        functools.partial(per_device, dims_of(mesh)),
        mesh=mesh,
        in_specs=in_specs,
        out_specs=out_specs,
        check_vma=False,
    )
```

```python
import functools

import jax
import jax.numpy as jnp
from jax import lax
from jax.experimental import pallas as pl
from jax.experimental.pallas import tpu as pltpu
from jax.sharding import PartitionSpec as P

MESH = pl.DeviceIdType.MESH
F32 = jnp.float32
BF16 = jnp.bfloat16
HIGHEST = lax.Precision.HIGHEST
K = 256
ROWS = 256
LANES = 128
PANEL = 64
PANELS = range(K // PANEL)
SUB = 8

NN = (((1,), (0,)), ((), ()))
NT = (((1,), (1,)), ((), ()))
TN = (((0,), (0,)), ((), ()))


def dims_of(mesh):
    pos, pix = mesh.shape["pos"], mesh.shape["pix"]
    nx = 4 if pos >= 16 else 2
    return nx, pos // (2 * nx), 2, pix


def spread(column):
    return jnp.broadcast_to(column, (SUB, 2 * PANEL))


def factor_panel(square):
    n = square.shape[0]
    at_row = lax.broadcasted_iota(jnp.int32, (n, n), 0)
    at_col = lax.broadcasted_iota(jnp.int32, (n, n), 1)
    eye = jnp.where(at_row == at_col, 1.0, 0.0).astype(F32)
    state = jnp.concatenate([square, eye], axis=1)
    groups = n // SUB
    rows = [state[SUB * g : SUB * (g + 1), :] for g in range(groups)]
    sub = lax.broadcasted_iota(jnp.int32, (SUB, 2 * n), 0)
    lane = lax.broadcasted_iota(jnp.int32, (SUB, 2 * n), 1)
    done = []
    for g in range(groups):
        at = SUB * g
        cols = {
            h: [spread(rows[h][:, at + k : at + k + 1]) for k in range(SUB)]
            for h in range(g, groups)
        }
        top, panel = rows[g], cols[g]
        pivots = jnp.ones((SUB, 2 * n), F32)
        for j in range(SUB):
            pivot = panel[j][j : j + 1, :]
            inverse = 1.0 / pivot
            pivots = jnp.where(sub == j, pivot, pivots)
            heads = [panel[k][j : j + 1, :] for k in range(SUB)]
            row = top[j : j + 1, :]
            under = jnp.where(sub > j, panel[j], 0.0)
            below = under * inverse
            for k in range(j + 1, SUB):
                term = (under * heads[k]) * inverse if k == j + 1 else below * heads[k]
                panel[k] = panel[k] - term
            top = top - below * row
            for h in range(g + 1, groups):
                scaled = cols[h][j] * inverse
                for k in range(j + 1, SUB):
                    cols[h][k] = cols[h][k] - scaled * heads[k]
                rows[h] = rows[h] - scaled * row
        done.append(jnp.where(lane >= sub + at, top * lax.rsqrt(pivots), 0.0))
    state = jnp.concatenate(done, axis=0)
    return state[:, :n], state[:, n:]


def split(value):
    high = value.astype(BF16)
    return high, (value - high.astype(F32)).astype(BF16)


def dot_split(a, b, numbers):
    a_high, a_low = split(a)
    b_high, b_low = split(b)
    dot = functools.partial(
        lax.dot_general, dimension_numbers=numbers, preferred_element_type=F32
    )
    return dot(a_high, b_high) + (dot(a_high, b_low) + dot(a_low, b_high))


def factorise(work, panels, size=K):
    for b in panels:
        lo, hi = b * PANEL, (b + 1) * PANEL
        upper, inverse = factor_panel(work[lo:hi, lo:hi])
        top = jnp.dot(inverse, work[lo:hi, :], precision=HIGHEST, preferred_element_type=F32)
        at_row = lax.broadcasted_iota(jnp.int32, top.shape, 0) + lo
        at_col = lax.broadcasted_iota(jnp.int32, top.shape, 1)
        top = jnp.where(at_col >= at_row, top, 0.0)
        work[lo:hi, :] = top
        if hi < size:
            work[hi:, :] -= lax.dot_general(
                top[:, hi:size], top, TN, precision=HIGHEST, preferred_element_type=F32
            )


def identity_beside(work, gram, size=K):
    at_row = lax.broadcasted_iota(jnp.int32, (size, size), 0)
    at_col = lax.broadcasted_iota(jnp.int32, (size, size), 1)
    work[:, :size] = gram
    work[:, size:] = jnp.where(at_row == at_col, 1.0, 0.0).astype(F32)


def sketch_kernel(
    dims,
    total,
    data_hbm,
    sketch_hbm,
    second_out,
    work_out,
    data,
    sketch,
    send_a,
    recv_a,
    own_a,
    first_t,
    recv_c,
    own_c,
    send_x,
    recv_x,
    send_z,
    recv_z,
    own_z,
    pair,
    loads,
    acc,
    recv_d,
    send_far,
    recv_far,
    parts,
    gsum,
    gathered,
    zparts,
    work,
    load_sem,
    sem_a,
    sem_f,
    sem_c,
    sem_x,
    sem_z,
    sem_p,
    sem_lz,
    sem_lx,
    sem_lc,
    sem_d,
    sem_s,
    sem_g,
):
    nx, nz, nc, ny = dims
    half = K // nc
    quarter = nz * LANES
    pos, y = lax.axis_index("pos"), lax.axis_index("pix")
    x, z, c = pos // (nz * nc), lax.rem(pos // nc, nz), lax.rem(pos, nc)
    group = nx * ny * nc
    mine = (x * ny + y) * nc + c
    share = K // group

    def at(px, pz, pc, py):
        return ((px * nz + pz) * nc + pc, py)

    def ahead(i, o, n):
        return lax.rem(i + o, n)

    def member(i):
        return at(i // (ny * nc), z, lax.rem(i, nc), lax.rem(i // nc, ny))

    def remote(src, dst, send_sem, recv_sem, device):
        return pltpu.make_async_remote_copy(
            src_ref=src,
            dst_ref=dst,
            send_sem=send_sem,
            recv_sem=recv_sem,
            device_id=device,
            device_id_type=MESH,
        )

    def rows_of(i):
        return pl.ds(pl.multiple_of(i * ROWS, ROWS), ROWS)

    def by_distance(n):
        return sorted(range(1, n), key=lambda o: (-min(o, n - o), o)) + [0]

    y_order, x_order, z_order = by_distance(ny), by_distance(nx), by_distance(nz)
    near_first = z_order[::-1]

    sketch_load = pltpu.make_async_copy(sketch_hbm, sketch, load_sem.at[ny])
    sketch_load.start()
    data_loads = []
    for o in y_order:
        rows = rows_of(ahead(y, o, ny))
        load = pltpu.make_async_copy(data_hbm.at[rows], data.at[rows], load_sem.at[o])
        load.start()
        data_loads.append(load)

    barrier = pltpu.get_barrier_semaphore()

    def greet_group(o, carry):
        pl.semaphore_signal(
            barrier, inc=1, device_id=member(ahead(mine, o, group)), device_id_type=MESH
        )
        return carry

    def greet_z(o, carry):
        pl.semaphore_signal(
            barrier, inc=1, device_id=at(x, ahead(z, o, nz), c, y), device_id_type=MESH
        )
        return carry

    lax.fori_loop(1, group, greet_group, 0, unroll=True)
    lax.fori_loop(1, nz, greet_z, 0, unroll=True)
    sketch_load.wait()

    copies_a = []
    for i, o in enumerate(y_order):
        data_loads[i].wait()
        block = jnp.dot(
            data[rows_of(ahead(y, o, ny)), :], sketch[...], preferred_element_type=F32
        )
        if o == 0:
            own_a[...] = block
        else:
            send_a[o - 1] = block.astype(BF16)
            if i == 0:
                pl.semaphore_wait(barrier, group - 1 + nz - 1)
            copy = remote(
                send_a.at[o - 1],
                recv_a.at[o - 1],
                sem_a.at[0, o - 1],
                sem_a.at[1, o - 1],
                at(x, z, c, ahead(y, o, ny)),
            )
            copy.start()
            copies_a.append(copy)
    first = own_a[...]
    for copy in copies_a:
        copy.wait_recv()
    for o in range(1, ny):
        first = first + recv_a[o - 1].astype(F32)
    mine_t = first.astype(BF16).T
    first_t[y] = mine_t
    copies_f = {}
    for o in y_order[:-1]:
        copy = remote(
            first_t.at[y],
            first_t.at[y],
            sem_f.at[0, o - 1],
            sem_f.at[1, o - 1],
            at(x, z, c, ahead(y, o, ny)),
        )
        copy.start()
        copies_f[o] = copy

    def wait_all(ref, sem):
        pltpu.make_async_copy(ref, ref, sem).wait()

    def gram_scatter(n):
        def step(o, carry):
            to = ahead(mine, o, group)
            remote(
                gsum.at[n, to],
                parts.at[n, o - 1],
                sem_g.at[n, 0, 0],
                sem_g.at[n, 0, 1],
                member(to),
            ).start()
            return carry

        lax.fori_loop(1, group, step, 0, unroll=True)

    def gram_across(n):
        others = parts.at[n, 0 : group - 1]
        wait_all(others, sem_g.at[n, 0, 1])
        zparts[n, 0] = gsum[n, mine] + jnp.sum(others[...], axis=0)

        def send(o, carry):
            remote(
                zparts.at[n, 0],
                zparts.at[n, o],
                sem_g.at[n, 1, 0],
                sem_g.at[n, 1, 1],
                at(x, ahead(z, o, nz), c, y),
            ).start()
            return carry

        lax.fori_loop(1, nz, send, 0, unroll=True)

    def gram_gather(n):
        wait_all(zparts.at[n, 1:nz], sem_g.at[n, 1, 1])

        def add(plane, sums):
            return sums + zparts[n, lax.rem(z - plane + nz, nz)]

        sums = lax.fori_loop(0, nz, add, jnp.zeros((share, K), F32), unroll=True)
        gathered[n, mine] = sums * (1.0 / total)

        def send(o, carry):
            remote(
                gathered.at[n, mine],
                gathered.at[n, mine],
                sem_g.at[n, 2, 0],
                sem_g.at[n, 2, 1],
                member(ahead(mine, o, group)),
            ).start()
            return carry

        lax.fori_loop(1, group, send, 0, unroll=True)

    def gram_done(n):
        wait_all(gathered.at[n, 0 : group - 1], sem_g.at[n, 2, 1])
        return gathered[n].reshape(K, K)

    def gram_sent(n):
        wait_all(parts.at[n, 0 : group - 1], sem_g.at[n, 0, 0])
        wait_all(zparts.at[n, 1:nz], sem_g.at[n, 1, 0])
        wait_all(gathered.at[n, 0 : group - 1], sem_g.at[n, 2, 0])

    gsum[0] = lax.dot_general(mine_t, mine_t, NT, preferred_element_type=F32).reshape(
        group, share, K
    )
    gram_scatter(0)

    def add_rows(offsets, i):
        xd = ahead(x, x_order[i], nx)

        def tile(t, carry):
            cols = pl.ds(pl.multiple_of(xd * quarter + t * ROWS, ROWS), ROWS)
            here = pl.ds(pl.multiple_of(t * ROWS, ROWS), ROWS)
            block = jnp.zeros((K, ROWS), F32)
            for o in offsets:
                block_at = lax.rem(y - o + ny, ny)
                block += jnp.dot(
                    first_t[block_at], data[rows_of(block_at), cols], preferred_element_type=F32
                )
            block = block.reshape(nc, half, ROWS)
            if 0 in offsets:
                own_c[i, :, :, here] = block
            else:
                own_c[i, :, :, here] += block
            return carry

        lax.fori_loop(0, quarter // ROWS, tile, 0)

    for i in range(nx):
        add_rows([0], i)
    for copy in copies_f.values():
        copy.wait_recv()
    gram_across(0)
    copies_c, copies_x = [], []
    for i in range(nx):
        add_rows(range(1, ny), i)
        copy = remote(
            own_c.at[i, 1 - c],
            recv_c.at[i],
            sem_c.at[0, i],
            sem_c.at[1, i],
            at(x, z, 1 - c, y),
        )
        copy.start()
        copies_c.append(copy)
    gram_gather(0)
    for i in range(nx - 1):
        copies_c[i].wait_recv()
        send_x[i] = (own_c[i, c] + recv_c[i]).astype(BF16)
        copy = remote(
            send_x.at[i],
            recv_x.at[i],
            sem_x.at[0, i],
            sem_x.at[1, i],
            at(ahead(x, x_order[i], nx), z, c, y),
        )
        copy.start()
        copies_x.append(copy)

    identity_beside(work, gram_done(0))
    factorise(work, PANELS[:3])

    last = nx - 1
    copies_c[last].wait_recv()
    for copy in copies_x:
        copy.wait_recv()
    copies_z = []
    for o in z_order:
        zd = ahead(z, o, nz)
        cols = pl.ds(pl.multiple_of(zd * LANES, LANES), LANES)
        block = own_c[last, c, :, cols] + recv_c[last, :, cols]
        for j in range(nx - 1):
            block = block + recv_x[j, :, cols].astype(F32)
        if o == 0:
            own_z[...] = block
        else:
            send_z[o - 1] = block.astype(BF16)
            copy = remote(
                send_z.at[o - 1],
                recv_z.at[o - 1],
                sem_z.at[0, o - 1],
                sem_z.at[1, o - 1],
                at(x, zd, c, y),
            )
            copy.start()
            copies_z.append(copy)
    factorise(work, PANELS[3:])
    block = own_z[...]
    for copy in copies_z:
        copy.wait_recv()
    for j in range(nz - 1):
        block = block + recv_z[j].astype(F32)
    pair[c] = block
    copy_p = remote(pair.at[c], pair.at[c], sem_p.at[0], sem_p.at[1], at(x, z, 1 - c, y))
    copy_p.start()
    copy_p.wait_recv()

    own_rows = pl.ds(pl.multiple_of(c * half, half), half)
    solved = dot_split(work[own_rows, K:], pair[...].reshape(K, LANES), NN)

    def cell(px, pz, pc):
        cols = pl.ds(pl.multiple_of((px * nz + pz) * LANES, LANES), LANES)
        return loads.at[pl.ds(pl.multiple_of(pc * half, half), half), cols]

    cell(x, z, c)[...] = (solved * (1.0 / total)).astype(BF16)

    def over_z(o):
        return remote(
            cell(x, z, c),
            cell(x, z, c),
            sem_lz.at[0, o],
            sem_lz.at[1, o],
            at(x, ahead(z, o, nz), c, y),
        )

    def over_x(ox, oz, hops):
        this = cell(lax.rem(x - ox + hops + nx, nx), lax.rem(z - oz + nz, nz), c)
        return remote(
            this,
            this,
            sem_lx.at[0, ox, oz],
            sem_lx.at[1, ox, oz],
            at(lax.rem(x + hops + nx, nx), z, c, y),
        )

    def over_c(ox):
        cols = pl.ds(pl.multiple_of(lax.rem(x - ox + nx, nx) * quarter, quarter), quarter)
        this = loads.at[own_rows, cols]
        return remote(this, this, sem_lc.at[0, ox], sem_lc.at[1, ox], at(x, z, 1 - c, y))

    for o in z_order[:-1]:
        over_z(o).start()
    steps = list(near_first)
    copies_lx = []

    def start_x(ox, oz, hops):
        copy = over_x(ox, oz, hops)
        copy.start()
        copies_lx.append(copy)

    for n in range(nz + 2):
        if n < nz:
            oz = steps[n]
            if oz > 0:
                over_z(oz).wait_recv()
            start_x(1, oz, 1)
            if nx > 2:
                start_x(nx - 1, oz, -1)
            if n == nz - 1:
                over_c(0).start()
        if n >= 2:
            oz = steps[n - 2]
            over_x(1, oz, 1).wait_recv()
            if nx == 4 and n % 2 == 0:
                start_x(2, oz, 1)
            if nx == 4:
                over_x(3, oz, -1).wait_recv()
                if n % 2 == 1:
                    start_x(2, oz, -1)

    over_c(1).start()
    if nx == 4:
        over_c(3).start()

    def add_pixels(ox):
        over_c(ox).wait_recv()
        cols = pl.ds(
            pl.multiple_of(lax.rem(x - ox + nx, nx) * quarter, quarter), quarter
        )
        copies = []
        for o in y_order:
            rows = rows_of(ahead(y, o, ny))
            term = lax.dot_general(data[rows, cols], loads[:, cols], NT, preferred_element_type=F32)
            if ox > 0:
                term = acc[o] + term
            if ox != nx // 2 or 2 * o != ny:
                acc[o] = term
            if ox == nx // 2 and o > 0:
                if 2 * o == ny:
                    send_far[...] = term.astype(BF16)
                copy = remote(
                    send_far if 2 * o == ny else acc.at[o],
                    recv_far if 2 * o == ny else recv_d.at[o - 1],
                    sem_d.at[0, o - 1],
                    sem_d.at[1, o - 1],
                    at(x, z, c, ahead(y, o, ny)),
                )
                copy.start()
                copies.append(copy)
        return copies

    add_pixels(0)
    if nx == 4:
        for n, oz in enumerate(steps):
            over_x(2, oz, 1 if n % 2 == 0 else -1).wait_recv()
        over_c(2).start()
        add_pixels(1)
        add_pixels(3)
    copies_d = add_pixels(nx // 2)
    mine_s = acc[0]
    for copy in copies_d:
        copy.wait_recv()
    for o in range(1, ny):
        mine_s = mine_s + (recv_far[...].astype(F32) if 2 * o == ny else recv_d[o - 1])
    second_out[y] = mine_s

    gsum[1] = lax.dot_general(
        mine_s, mine_s, TN, precision=HIGHEST, preferred_element_type=F32
    ).reshape(group, share, K)
    gram_scatter(1)
    gram_across(1)
    gram_gather(1)
    copies_s = []
    for o in y_order[:-1]:
        copy = remote(
            second_out.at[y],
            second_out.at[y],
            sem_s.at[0, o - 1],
            sem_s.at[1, o - 1],
            at(x, z, c, ahead(y, o, ny)),
        )
        copy.start()
        copies_s.append(copy)

    copies = copies_a + list(copies_f.values()) + copies_c + copies_x + copies_z + copies_d
    for copy in copies + copies_lx + [copy_p]:
        copy.wait_send()
    for oz in range(1, nz):
        over_z(oz).wait_send()
    for ox in range(nx):
        over_c(ox).wait_send()
    gram_sent(0)

    identity_beside(work_out, gram_done(1))
    factorise(work_out, PANELS)
    gram_sent(1)
    for copy in copies_s:
        copy.wait()


def basis_kernel(second, work, basis, factor):
    for q in range(second.shape[0]):
        basis[q * ROWS : (q + 1) * ROWS, :] = dot_split(second[q], work[:, K:], NT)
    factor[...] = work[:, :K]


def per_device(dims, data, sketch_matrix):
    nx, nz, nc, ny = dims
    rows, pixels = data.shape
    total = rows * nx * nz * nc
    half, quarter, group = K // nc, nz * LANES, nx * ny * nc
    share = K // group
    assert rows == ny * ROWS and pixels == nx * quarter
    vm = pltpu.VMEM
    dma = pltpu.SemaphoreType.DMA
    second, work = pl.pallas_call(
        functools.partial(sketch_kernel, dims, total),
        out_shape=(
            jax.ShapeDtypeStruct((ny, ROWS, K), F32),
            jax.ShapeDtypeStruct((K, 2 * K), F32),
        ),
        in_specs=[pl.BlockSpec(memory_space=pl.ANY)] * 2,
        out_specs=(pl.BlockSpec(memory_space=pltpu.VMEM),) * 2,
        scratch_shapes=[
            vm((rows, pixels), BF16),
            vm((pixels, K), BF16),
            vm((ny - 1, ROWS, K), BF16),
            vm((ny - 1, ROWS, K), BF16),
            vm((ROWS, K), F32),
            vm((ny, K, ROWS), BF16),
            vm((nx, half, quarter), F32),
            vm((nx, nc, half, quarter), F32),
            vm((nx - 1, half, quarter), BF16),
            vm((nx - 1, half, quarter), BF16),
            vm((nz - 1, half, LANES), BF16),
            vm((nz - 1, half, LANES), BF16),
            vm((half, LANES), F32),
            vm((nc, half, LANES), F32),
            vm((K, pixels), BF16),
            vm((ny, ROWS, K), F32),
            vm((ny - 1, ROWS, K), F32),
            vm((ROWS, K), BF16),
            vm((ROWS, K), BF16),
            vm((2, group, share, K), F32),
            vm((2, group, share, K), F32),
            vm((2, group, share, K), F32),
            vm((2, nz, share, K), F32),
            vm((K, 2 * K), F32),
            dma((ny + 1,)),
            dma((2, ny - 1)),
            dma((2, ny - 1)),
            dma((2, nx)),
            dma((2, nx - 1)),
            dma((2, nz - 1)),
            dma((2,)),
            dma((2, nz)),
            dma((2, nx, nz)),
            dma((2, nx)),
            dma((2, ny - 1)),
            dma((2, ny - 1)),
            dma((2, 3, 2)),
        ],
        compiler_params=pltpu.CompilerParams(
            collective_id=0, has_side_effects=True, vmem_limit_bytes=60 * 1024 * 1024
        ),
        cost_estimate=pl.CostEstimate(
            flops=6 * rows * pixels * K, bytes_accessed=2 * rows * pixels, transcendentals=0
        ),
        name="sketch",
    )(data, sketch_matrix)
    return pl.pallas_call(
        basis_kernel,
        grid=(2,),
        out_shape=(
            jax.ShapeDtypeStruct((rows, K), F32),
            jax.ShapeDtypeStruct((K, K), F32),
        ),
        in_specs=[
            pl.BlockSpec((ny // 2, ROWS, K), lambda q: (q, 0, 0)),
            pl.BlockSpec((K, 2 * K), lambda q: (0, 0)),
        ],
        out_specs=(
            pl.BlockSpec((rows // 2, K), lambda q: (q, 0)),
            pl.BlockSpec((K, K), lambda q: (0, 0)),
        ),
        compiler_params=pltpu.CompilerParams(vmem_limit_bytes=60 * 1024 * 1024),
        name="basis",
    )(second, work)


def solution(mesh):
    in_specs = (P("pos", "pix"), P("pix", None))
    out_specs = (P("pos", None), P())
    return jax.shard_map(
        functools.partial(per_device, dims_of(mesh)),
        mesh=mesh,
        in_specs=in_specs,
        out_specs=out_specs,
        check_vma=False,
    )
```

```python
import functools

import jax
import jax.numpy as jnp
from jax import lax
from jax.experimental import pallas as pl
from jax.experimental.pallas import tpu as pltpu
from jax.sharding import PartitionSpec as P

MESH = pl.DeviceIdType.MESH
F32 = jnp.float32
BF16 = jnp.bfloat16
HIGHEST = lax.Precision.HIGHEST
K = 256
ROWS = 256
LANES = 128
PANEL = 64
PANELS = range(K // PANEL)
SUB = 8

NN = (((1,), (0,)), ((), ()))
NT = (((1,), (1,)), ((), ()))
TN = (((0,), (0,)), ((), ()))


def dims_of(mesh):
    pos, pix = mesh.shape["pos"], mesh.shape["pix"]
    nx = 4 if pos >= 16 else 2
    return nx, pos // (2 * nx), 2, pix


def spread(column):
    return jnp.broadcast_to(column, (SUB, 2 * PANEL))


def factor_panel(square):
    n = square.shape[0]
    at_row = lax.broadcasted_iota(jnp.int32, (n, n), 0)
    at_col = lax.broadcasted_iota(jnp.int32, (n, n), 1)
    eye = jnp.where(at_row == at_col, 1.0, 0.0).astype(F32)
    state = jnp.concatenate([square, eye], axis=1)
    groups = n // SUB
    rows = [state[SUB * g : SUB * (g + 1), :] for g in range(groups)]
    sub = lax.broadcasted_iota(jnp.int32, (SUB, 2 * n), 0)
    lane = lax.broadcasted_iota(jnp.int32, (SUB, 2 * n), 1)
    done = []
    for g in range(groups):
        at = SUB * g
        cols = {
            h: [spread(rows[h][:, at + k : at + k + 1]) for k in range(SUB)]
            for h in range(g, groups)
        }
        top, panel = rows[g], cols[g]
        pivots = jnp.ones((SUB, 2 * n), F32)
        for j in range(SUB):
            pivot = panel[j][j : j + 1, :]
            inverse = 1.0 / pivot
            pivots = jnp.where(sub == j, pivot, pivots)
            heads = [panel[k][j : j + 1, :] for k in range(SUB)]
            row = top[j : j + 1, :]
            under = jnp.where(sub > j, panel[j], 0.0)
            below = under * inverse
            for k in range(j + 1, SUB):
                term = (under * heads[k]) * inverse if k == j + 1 else below * heads[k]
                panel[k] = panel[k] - term
            top = top - below * row
            for h in range(g + 1, groups):
                scaled = cols[h][j] * inverse
                for k in range(j + 1, SUB):
                    cols[h][k] = cols[h][k] - scaled * heads[k]
                rows[h] = rows[h] - scaled * row
        done.append(jnp.where(lane >= sub + at, top * lax.rsqrt(pivots), 0.0))
    state = jnp.concatenate(done, axis=0)
    return state[:, :n], state[:, n:]


def split(value):
    high = value.astype(BF16)
    return high, (value - high.astype(F32)).astype(BF16)


def dot_split(a, b, numbers):
    a_high, a_low = split(a)
    b_high, b_low = split(b)
    dot = functools.partial(
        lax.dot_general, dimension_numbers=numbers, preferred_element_type=F32
    )
    return dot(a_high, b_high) + (dot(a_high, b_low) + dot(a_low, b_high))


def factorise(work, panels, size=K):
    square = None
    for b in panels:
        lo, hi = b * PANEL, (b + 1) * PANEL
        if square is None:
            square = work[lo:hi, lo:hi]
        upper, inverse = factor_panel(square)
        left, right = lo // LANES * LANES, size + -(-hi // LANES) * LANES
        top = jnp.dot(
            inverse, work[lo:hi, left:right], precision=HIGHEST, preferred_element_type=F32
        )
        at_row = lax.broadcasted_iota(jnp.int32, top.shape, 0) + lo
        at_col = lax.broadcasted_iota(jnp.int32, top.shape, 1) + left
        top = jnp.where(at_col >= at_row, top, 0.0)
        if hi < size:
            ahead = top[:, hi - left : hi + PANEL - left]
            square = work[hi : hi + PANEL, hi : hi + PANEL] - lax.dot_general(
                ahead, ahead, TN, precision=HIGHEST, preferred_element_type=F32
            )
            work[hi:, left:right] -= lax.dot_general(
                top[:, hi - left : size - left],
                top,
                TN,
                precision=HIGHEST,
                preferred_element_type=F32,
            )
        if left > 0:
            work[lo:hi, :left] = jnp.zeros((PANEL, left), F32)
        work[lo:hi, left:right] = top
        if right < 2 * size:
            work[lo:hi, right:] = jnp.zeros((PANEL, 2 * size - right), F32)


def identity_beside(work, gram, size=K):
    at_row = lax.broadcasted_iota(jnp.int32, (size, size), 0)
    at_col = lax.broadcasted_iota(jnp.int32, (size, size), 1)
    work[:, :size] = gram
    work[:, size:] = jnp.where(at_row == at_col, 1.0, 0.0).astype(F32)


def sketch_kernel(
    dims,
    total,
    data_hbm,
    sketch_hbm,
    second_out,
    work_out,
    data,
    sketch,
    send_a,
    recv_a,
    own_a,
    first_t,
    recv_c,
    own_c,
    send_x,
    recv_x,
    send_z,
    recv_z,
    own_z,
    pair,
    loads,
    acc,
    recv_d,
    send_far,
    recv_far,
    parts,
    gsum,
    gathered,
    zparts,
    work,
    load_sem,
    sem_a,
    sem_f,
    sem_c,
    sem_x,
    sem_z,
    sem_p,
    sem_lz,
    sem_lx,
    sem_lc,
    sem_d,
    sem_s,
    sem_g,
):
    nx, nz, nc, ny = dims
    half = K // nc
    quarter = nz * LANES
    pos, y = lax.axis_index("pos"), lax.axis_index("pix")
    x, z, c = pos // (nz * nc), lax.rem(pos // nc, nz), lax.rem(pos, nc)
    group = nx * ny * nc
    mine = (x * ny + y) * nc + c
    share = K // group

    def at(px, pz, pc, py):
        return ((px * nz + pz) * nc + pc, py)

    def ahead(i, o, n):
        return lax.rem(i + o, n)

    def member(i):
        return at(i // (ny * nc), z, lax.rem(i, nc), lax.rem(i // nc, ny))

    def remote(src, dst, send_sem, recv_sem, device):
        return pltpu.make_async_remote_copy(
            src_ref=src,
            dst_ref=dst,
            send_sem=send_sem,
            recv_sem=recv_sem,
            device_id=device,
            device_id_type=MESH,
        )

    def rows_of(i):
        return pl.ds(pl.multiple_of(i * ROWS, ROWS), ROWS)

    def by_distance(n):
        return sorted(range(1, n), key=lambda o: (-min(o, n - o), o)) + [0]

    y_order, x_order, z_order = by_distance(ny), by_distance(nx), by_distance(nz)
    near_first = z_order[::-1]

    sketch_load = pltpu.make_async_copy(sketch_hbm, sketch, load_sem.at[ny])
    sketch_load.start()
    data_loads = []
    for o in y_order:
        rows = rows_of(ahead(y, o, ny))
        load = pltpu.make_async_copy(data_hbm.at[rows], data.at[rows], load_sem.at[o])
        load.start()
        data_loads.append(load)

    barrier = pltpu.get_barrier_semaphore()

    def greet_group(o, carry):
        pl.semaphore_signal(
            barrier, inc=1, device_id=member(ahead(mine, o, group)), device_id_type=MESH
        )
        return carry

    def greet_z(o, carry):
        pl.semaphore_signal(
            barrier, inc=1, device_id=at(x, ahead(z, o, nz), c, y), device_id_type=MESH
        )
        return carry

    lax.fori_loop(1, group, greet_group, 0, unroll=True)
    lax.fori_loop(1, nz, greet_z, 0, unroll=True)
    sketch_load.wait()

    copies_a = []
    for i, o in enumerate(y_order):
        data_loads[i].wait()
        block = jnp.dot(
            data[rows_of(ahead(y, o, ny)), :], sketch[...], preferred_element_type=F32
        )
        if o == 0:
            own_a[...] = block
        else:
            send_a[o - 1] = block.astype(BF16)
            if i == 0:
                pl.semaphore_wait(barrier, group - 1 + nz - 1)
            copy = remote(
                send_a.at[o - 1],
                recv_a.at[o - 1],
                sem_a.at[0, o - 1],
                sem_a.at[1, o - 1],
                at(x, z, c, ahead(y, o, ny)),
            )
            copy.start()
            copies_a.append(copy)
    first = own_a[...]
    for copy in copies_a:
        copy.wait_recv()
    for o in range(1, ny):
        first = first + recv_a[o - 1].astype(F32)
    mine_t = first.astype(BF16).T
    first_t[y] = mine_t
    copies_f = {}
    for o in y_order[:-1]:
        copy = remote(
            first_t.at[y],
            first_t.at[y],
            sem_f.at[0, o - 1],
            sem_f.at[1, o - 1],
            at(x, z, c, ahead(y, o, ny)),
        )
        copy.start()
        copies_f[o] = copy

    def wait_all(ref, sem):
        pltpu.make_async_copy(ref, ref, sem).wait()

    def gram_scatter(n):
        def step(o, carry):
            to = ahead(mine, o, group)
            remote(
                gsum.at[n, to],
                parts.at[n, o - 1],
                sem_g.at[n, 0, 0],
                sem_g.at[n, 0, 1],
                member(to),
            ).start()
            return carry

        lax.fori_loop(1, group, step, 0, unroll=True)

    def gram_across(n):
        others = parts.at[n, 0 : group - 1]
        wait_all(others, sem_g.at[n, 0, 1])
        zparts[n, 0] = gsum[n, mine] + jnp.sum(others[...], axis=0)

        def send(o, carry):
            remote(
                zparts.at[n, 0],
                zparts.at[n, o],
                sem_g.at[n, 1, 0],
                sem_g.at[n, 1, 1],
                at(x, ahead(z, o, nz), c, y),
            ).start()
            return carry

        lax.fori_loop(1, nz, send, 0, unroll=True)

    def gram_gather(n):
        wait_all(zparts.at[n, 1:nz], sem_g.at[n, 1, 1])

        def add(plane, sums):
            return sums + zparts[n, lax.rem(z - plane + nz, nz)]

        sums = lax.fori_loop(0, nz, add, jnp.zeros((share, K), F32), unroll=True)
        gathered[n, mine] = sums * (1.0 / total)

        def send(o, carry):
            remote(
                gathered.at[n, mine],
                gathered.at[n, mine],
                sem_g.at[n, 2, 0],
                sem_g.at[n, 2, 1],
                member(ahead(mine, o, group)),
            ).start()
            return carry

        lax.fori_loop(1, group, send, 0, unroll=True)

    def gram_done(n):
        wait_all(gathered.at[n, 0 : group - 1], sem_g.at[n, 2, 1])
        return gathered[n].reshape(K, K)

    def gram_sent(n):
        wait_all(parts.at[n, 0 : group - 1], sem_g.at[n, 0, 0])
        wait_all(zparts.at[n, 1:nz], sem_g.at[n, 1, 0])
        wait_all(gathered.at[n, 0 : group - 1], sem_g.at[n, 2, 0])

    gsum[0] = lax.dot_general(mine_t, mine_t, NT, preferred_element_type=F32).reshape(
        group, share, K
    )
    gram_scatter(0)

    def add_rows(offsets, i):
        xd = ahead(x, x_order[i], nx)

        def tile(t, carry):
            cols = pl.ds(pl.multiple_of(xd * quarter + t * ROWS, ROWS), ROWS)
            here = pl.ds(pl.multiple_of(t * ROWS, ROWS), ROWS)
            block = jnp.zeros((K, ROWS), F32)
            for o in offsets:
                block_at = lax.rem(y - o + ny, ny)
                block += jnp.dot(
                    first_t[block_at], data[rows_of(block_at), cols], preferred_element_type=F32
                )
            block = block.reshape(nc, half, ROWS)
            if 0 in offsets:
                own_c[i, :, :, here] = block
            else:
                own_c[i, :, :, here] += block
            return carry

        lax.fori_loop(0, quarter // ROWS, tile, 0)

    for i in range(nx):
        add_rows([0], i)
    for copy in copies_f.values():
        copy.wait_recv()
    gram_across(0)
    copies_c, copies_x = [], []
    for i in range(nx):
        add_rows(range(1, ny), i)
        copy = remote(
            own_c.at[i, 1 - c],
            recv_c.at[i],
            sem_c.at[0, i],
            sem_c.at[1, i],
            at(x, z, 1 - c, y),
        )
        copy.start()
        copies_c.append(copy)
    gram_gather(0)
    for i in range(nx - 1):
        copies_c[i].wait_recv()
        send_x[i] = (own_c[i, c] + recv_c[i]).astype(BF16)
        copy = remote(
            send_x.at[i],
            recv_x.at[i],
            sem_x.at[0, i],
            sem_x.at[1, i],
            at(ahead(x, x_order[i], nx), z, c, y),
        )
        copy.start()
        copies_x.append(copy)

    identity_beside(work, gram_done(0))
    factorise(work, PANELS[:3])

    last = nx - 1
    copies_c[last].wait_recv()
    for copy in copies_x:
        copy.wait_recv()
    copies_z = []
    for o in z_order:
        zd = ahead(z, o, nz)
        cols = pl.ds(pl.multiple_of(zd * LANES, LANES), LANES)
        block = own_c[last, c, :, cols] + recv_c[last, :, cols]
        for j in range(nx - 1):
            block = block + recv_x[j, :, cols].astype(F32)
        if o == 0:
            own_z[...] = block
        else:
            send_z[o - 1] = block.astype(BF16)
            copy = remote(
                send_z.at[o - 1],
                recv_z.at[o - 1],
                sem_z.at[0, o - 1],
                sem_z.at[1, o - 1],
                at(x, zd, c, y),
            )
            copy.start()
            copies_z.append(copy)
    factorise(work, PANELS[3:])
    block = own_z[...]
    for copy in copies_z:
        copy.wait_recv()
    for j in range(nz - 1):
        block = block + recv_z[j].astype(F32)
    pair[c] = block
    copy_p = remote(pair.at[c], pair.at[c], sem_p.at[0], sem_p.at[1], at(x, z, 1 - c, y))
    copy_p.start()
    copy_p.wait_recv()

    own_rows = pl.ds(pl.multiple_of(c * half, half), half)
    solved = dot_split(work[own_rows, K:], pair[...].reshape(K, LANES), NN)

    def cell(px, pz, pc):
        cols = pl.ds(pl.multiple_of((px * nz + pz) * LANES, LANES), LANES)
        return loads.at[pl.ds(pl.multiple_of(pc * half, half), half), cols]

    cell(x, z, c)[...] = (solved * (1.0 / total)).astype(BF16)

    def over_z(o):
        return remote(
            cell(x, z, c),
            cell(x, z, c),
            sem_lz.at[0, o],
            sem_lz.at[1, o],
            at(x, ahead(z, o, nz), c, y),
        )

    def over_x(ox, oz, hops):
        this = cell(lax.rem(x - ox + hops + nx, nx), lax.rem(z - oz + nz, nz), c)
        return remote(
            this,
            this,
            sem_lx.at[0, ox, oz],
            sem_lx.at[1, ox, oz],
            at(lax.rem(x + hops + nx, nx), z, c, y),
        )

    def over_c(ox):
        cols = pl.ds(pl.multiple_of(lax.rem(x - ox + nx, nx) * quarter, quarter), quarter)
        this = loads.at[own_rows, cols]
        return remote(this, this, sem_lc.at[0, ox], sem_lc.at[1, ox], at(x, z, 1 - c, y))

    for o in z_order[:-1]:
        over_z(o).start()
    steps = list(near_first)
    copies_lx = []

    def start_x(ox, oz, hops):
        copy = over_x(ox, oz, hops)
        copy.start()
        copies_lx.append(copy)

    relayed = nz - 3
    for n in range(nz + 2):
        if n < nz:
            oz = steps[n]
            if oz > 0:
                over_z(oz).wait_recv()
            start_x(1, oz, 1)
            if nx > 2:
                start_x(nx - 1, oz, -1)
            if nx == 4 and n >= relayed:
                start_x(2, oz, 2)
            if n == nz - 1:
                over_c(0).start()
        if n >= 2:
            oz = steps[n - 2]
            over_x(1, oz, 1).wait_recv()
            if nx == 4 and n - 2 < relayed and n % 2 == 0:
                start_x(2, oz, 1)
            if nx == 4:
                over_x(3, oz, -1).wait_recv()
                if n - 2 < relayed and n % 2 == 1:
                    start_x(2, oz, -1)

    over_c(1).start()
    if nx == 4:
        over_c(3).start()

    def add_pixels(ox):
        over_c(ox).wait_recv()
        cols = pl.ds(
            pl.multiple_of(lax.rem(x - ox + nx, nx) * quarter, quarter), quarter
        )
        copies = []
        for o in y_order:
            rows = rows_of(ahead(y, o, ny))
            term = lax.dot_general(data[rows, cols], loads[:, cols], NT, preferred_element_type=F32)
            if ox > 0:
                term = acc[o] + term
            if ox != nx // 2 or 2 * o != ny:
                acc[o] = term
            if ox == nx // 2 and o > 0:
                if 2 * o == ny:
                    send_far[...] = term.astype(BF16)
                copy = remote(
                    send_far if 2 * o == ny else acc.at[o],
                    recv_far if 2 * o == ny else recv_d.at[o - 1],
                    sem_d.at[0, o - 1],
                    sem_d.at[1, o - 1],
                    at(x, z, c, ahead(y, o, ny)),
                )
                copy.start()
                copies.append(copy)
        return copies

    add_pixels(0)
    if nx == 4:
        for n, oz in enumerate(steps):
            over_x(2, oz, 1 if n % 2 == 0 else -1).wait_recv()
        over_c(2).start()
        add_pixels(1)
        add_pixels(3)
    copies_d = add_pixels(nx // 2)
    mine_s = acc[0]
    for copy in copies_d:
        copy.wait_recv()
    for o in range(1, ny):
        mine_s = mine_s + (recv_far[...].astype(F32) if 2 * o == ny else recv_d[o - 1])
    second_out[y] = mine_s

    gsum[1] = lax.dot_general(
        mine_s, mine_s, TN, precision=HIGHEST, preferred_element_type=F32
    ).reshape(group, share, K)
    gram_scatter(1)
    gram_across(1)
    gram_gather(1)
    copies_s = []
    for o in y_order[:-1]:
        copy = remote(
            second_out.at[y],
            second_out.at[y],
            sem_s.at[0, o - 1],
            sem_s.at[1, o - 1],
            at(x, z, c, ahead(y, o, ny)),
        )
        copy.start()
        copies_s.append(copy)

    copies = copies_a + list(copies_f.values()) + copies_c + copies_x + copies_z + copies_d
    for copy in copies + copies_lx + [copy_p]:
        copy.wait_send()
    for oz in range(1, nz):
        over_z(oz).wait_send()
    for ox in range(nx):
        over_c(ox).wait_send()
    gram_sent(0)

    identity_beside(work_out, gram_done(1))
    factorise(work_out, PANELS)
    gram_sent(1)
    for copy in copies_s:
        copy.wait()


def basis_kernel(second, work, basis, factor):
    for q in range(second.shape[0]):
        basis[q * ROWS : (q + 1) * ROWS, :] = dot_split(second[q], work[:, K:], NT)
    factor[...] = work[:, :K]


def per_device(dims, data, sketch_matrix):
    nx, nz, nc, ny = dims
    rows, pixels = data.shape
    total = rows * nx * nz * nc
    half, quarter, group = K // nc, nz * LANES, nx * ny * nc
    share = K // group
    assert rows == ny * ROWS and pixels == nx * quarter
    vm = pltpu.VMEM
    dma = pltpu.SemaphoreType.DMA
    second, work = pl.pallas_call(
        functools.partial(sketch_kernel, dims, total),
        out_shape=(
            jax.ShapeDtypeStruct((ny, ROWS, K), F32),
            jax.ShapeDtypeStruct((K, 2 * K), F32),
        ),
        in_specs=[pl.BlockSpec(memory_space=pl.ANY)] * 2,
        out_specs=(pl.BlockSpec(memory_space=pltpu.VMEM),) * 2,
        scratch_shapes=[
            vm((rows, pixels), BF16),
            vm((pixels, K), BF16),
            vm((ny - 1, ROWS, K), BF16),
            vm((ny - 1, ROWS, K), BF16),
            vm((ROWS, K), F32),
            vm((ny, K, ROWS), BF16),
            vm((nx, half, quarter), F32),
            vm((nx, nc, half, quarter), F32),
            vm((nx - 1, half, quarter), BF16),
            vm((nx - 1, half, quarter), BF16),
            vm((nz - 1, half, LANES), BF16),
            vm((nz - 1, half, LANES), BF16),
            vm((half, LANES), F32),
            vm((nc, half, LANES), F32),
            vm((K, pixels), BF16),
            vm((ny, ROWS, K), F32),
            vm((ny - 1, ROWS, K), F32),
            vm((ROWS, K), BF16),
            vm((ROWS, K), BF16),
            vm((2, group, share, K), F32),
            vm((2, group, share, K), F32),
            vm((2, group, share, K), F32),
            vm((2, nz, share, K), F32),
            vm((K, 2 * K), F32),
            dma((ny + 1,)),
            dma((2, ny - 1)),
            dma((2, ny - 1)),
            dma((2, nx)),
            dma((2, nx - 1)),
            dma((2, nz - 1)),
            dma((2,)),
            dma((2, nz)),
            dma((2, nx, nz)),
            dma((2, nx)),
            dma((2, ny - 1)),
            dma((2, ny - 1)),
            dma((2, 3, 2)),
        ],
        compiler_params=pltpu.CompilerParams(
            collective_id=0, has_side_effects=True, vmem_limit_bytes=60 * 1024 * 1024
        ),
        cost_estimate=pl.CostEstimate(
            flops=6 * rows * pixels * K, bytes_accessed=2 * rows * pixels, transcendentals=0
        ),
        name="sketch",
    )(data, sketch_matrix)
    return pl.pallas_call(
        basis_kernel,
        grid=(2,),
        out_shape=(
            jax.ShapeDtypeStruct((rows, K), F32),
            jax.ShapeDtypeStruct((K, K), F32),
        ),
        in_specs=[
            pl.BlockSpec((ny // 2, ROWS, K), lambda q: (q, 0, 0)),
            pl.BlockSpec((K, 2 * K), lambda q: (0, 0)),
        ],
        out_specs=(
            pl.BlockSpec((rows // 2, K), lambda q: (q, 0)),
            pl.BlockSpec((K, K), lambda q: (0, 0)),
        ),
        compiler_params=pltpu.CompilerParams(vmem_limit_bytes=60 * 1024 * 1024),
        name="basis",
    )(second, work)


def solution(mesh):
    in_specs = (P("pos", "pix"), P("pix", None))
    out_specs = (P("pos", None), P())
    return jax.shard_map(
        functools.partial(per_device, dims_of(mesh)),
        mesh=mesh,
        in_specs=in_specs,
        out_specs=out_specs,
        check_vma=False,
    )
```

```python
import functools

import jax
import jax.numpy as jnp
from jax import lax
from jax.experimental import pallas as pl
from jax.experimental.pallas import tpu as pltpu
from jax.sharding import PartitionSpec as P

MESH = pl.DeviceIdType.MESH
F32 = jnp.float32
BF16 = jnp.bfloat16
HIGHEST = lax.Precision.HIGHEST
K = 256
ROWS = 256
LANES = 128
PANEL = 64
PANELS = range(K // PANEL)
SUB = 8

NN = (((1,), (0,)), ((), ()))
NT = (((1,), (1,)), ((), ()))
TN = (((0,), (0,)), ((), ()))


def dims_of(mesh):
    pos, pix = mesh.shape["pos"], mesh.shape["pix"]
    nx = 4 if pos >= 16 else 2
    return nx, pos // (2 * nx), 2, pix


def spread(column):
    return jnp.broadcast_to(column, (SUB, 2 * PANEL))


def factor_panel(square):
    n = square.shape[0]
    at_row = lax.broadcasted_iota(jnp.int32, (n, n), 0)
    at_col = lax.broadcasted_iota(jnp.int32, (n, n), 1)
    eye = jnp.where(at_row == at_col, 1.0, 0.0).astype(F32)
    state = jnp.concatenate([square, eye], axis=1)
    groups = n // SUB
    rows = [state[SUB * g : SUB * (g + 1), :] for g in range(groups)]
    sub = lax.broadcasted_iota(jnp.int32, (SUB, 2 * n), 0)
    lane = lax.broadcasted_iota(jnp.int32, (SUB, 2 * n), 1)
    done = []
    for g in range(groups):
        at = SUB * g
        cols = {
            h: [spread(rows[h][:, at + k : at + k + 1]) for k in range(SUB)]
            for h in range(g, groups)
        }
        top, panel = rows[g], cols[g]
        pivots = jnp.ones((SUB, 2 * n), F32)
        for j in range(SUB):
            pivot = panel[j][j : j + 1, :]
            inverse = 1.0 / pivot
            pivots = jnp.where(sub == j, pivot, pivots)
            heads = [panel[k][j : j + 1, :] for k in range(SUB)]
            row = top[j : j + 1, :]
            under = jnp.where(sub > j, panel[j], 0.0)
            below = under * inverse
            for k in range(j + 1, SUB):
                term = (under * heads[k]) * inverse if k == j + 1 else below * heads[k]
                panel[k] = panel[k] - term
            top = top - below * row
            for h in range(g + 1, groups):
                scaled = cols[h][j] * inverse
                for k in range(j + 1, SUB):
                    cols[h][k] = cols[h][k] - scaled * heads[k]
                rows[h] = rows[h] - scaled * row
        done.append(jnp.where(lane >= sub + at, top * lax.rsqrt(pivots), 0.0))
    state = jnp.concatenate(done, axis=0)
    return state[:, :n], state[:, n:]


def split(value):
    high = value.astype(BF16)
    return high, (value - high.astype(F32)).astype(BF16)


def dot_split(a, b, numbers):
    a_high, a_low = split(a)
    b_high, b_low = split(b)
    dot = functools.partial(
        lax.dot_general, dimension_numbers=numbers, preferred_element_type=F32
    )
    return dot(a_high, b_high) + (dot(a_high, b_low) + dot(a_low, b_high))


def factorise(work, panels, size=K):
    square = None
    for b in panels:
        lo, hi = b * PANEL, (b + 1) * PANEL
        if square is None:
            square = work[lo:hi, lo:hi]
        upper, inverse = factor_panel(square)
        left, right = lo // LANES * LANES, size + -(-hi // LANES) * LANES
        top = jnp.dot(
            inverse, work[lo:hi, left:right], precision=HIGHEST, preferred_element_type=F32
        )
        at_row = lax.broadcasted_iota(jnp.int32, top.shape, 0) + lo
        at_col = lax.broadcasted_iota(jnp.int32, top.shape, 1) + left
        top = jnp.where(at_col >= at_row, top, 0.0)
        if hi < size:
            ahead = top[:, hi - left : hi + PANEL - left]
            square = work[hi : hi + PANEL, hi : hi + PANEL] - lax.dot_general(
                ahead, ahead, TN, precision=HIGHEST, preferred_element_type=F32
            )
            work[hi:, left:right] -= lax.dot_general(
                top[:, hi - left : size - left],
                top,
                TN,
                precision=HIGHEST,
                preferred_element_type=F32,
            )
        if left > 0:
            work[lo:hi, :left] = jnp.zeros((PANEL, left), F32)
        work[lo:hi, left:right] = top
        if right < 2 * size:
            work[lo:hi, right:] = jnp.zeros((PANEL, 2 * size - right), F32)


def identity_beside(work, gram, size=K):
    at_row = lax.broadcasted_iota(jnp.int32, (size, size), 0)
    at_col = lax.broadcasted_iota(jnp.int32, (size, size), 1)
    work[:, :size] = gram
    work[:, size:] = jnp.where(at_row == at_col, 1.0, 0.0).astype(F32)


def sketch_kernel(
    dims,
    total,
    data_hbm,
    sketch_hbm,
    second_out,
    work_out,
    data,
    sketch,
    send_a,
    recv_a,
    own_a,
    first_t,
    recv_c,
    own_c,
    send_x,
    recv_x,
    send_z,
    recv_z,
    own_z,
    pair,
    loads,
    acc,
    recv_d,
    send_far,
    recv_far,
    parts,
    gsum,
    gathered,
    zparts,
    work,
    load_sem,
    sem_a,
    sem_f,
    sem_c,
    sem_x,
    sem_z,
    sem_p,
    sem_lz,
    sem_lx,
    sem_lc,
    sem_d,
    sem_s,
    sem_g,
):
    nx, nz, nc, ny = dims
    half = K // nc
    quarter = nz * LANES
    pos, y = lax.axis_index("pos"), lax.axis_index("pix")
    x, z, c = pos // (nz * nc), lax.rem(pos // nc, nz), lax.rem(pos, nc)
    group = nx * ny * nc
    mine = (x * ny + y) * nc + c
    share = K // group

    def at(px, pz, pc, py):
        return ((px * nz + pz) * nc + pc, py)

    def ahead(i, o, n):
        return lax.rem(i + o, n)

    def member(i):
        return at(i // (ny * nc), z, lax.rem(i, nc), lax.rem(i // nc, ny))

    def remote(src, dst, send_sem, recv_sem, device):
        return pltpu.make_async_remote_copy(
            src_ref=src,
            dst_ref=dst,
            send_sem=send_sem,
            recv_sem=recv_sem,
            device_id=device,
            device_id_type=MESH,
        )

    def rows_of(i):
        return pl.ds(pl.multiple_of(i * ROWS, ROWS), ROWS)

    def by_distance(n):
        return sorted(range(1, n), key=lambda o: (-min(o, n - o), o)) + [0]

    y_order, x_order, z_order = by_distance(ny), by_distance(nx), by_distance(nz)
    near_first = z_order[::-1]

    sketch_load = pltpu.make_async_copy(sketch_hbm, sketch, load_sem.at[ny])
    sketch_load.start()
    data_loads = []
    for o in y_order:
        rows = rows_of(ahead(y, o, ny))
        load = pltpu.make_async_copy(data_hbm.at[rows], data.at[rows], load_sem.at[o])
        load.start()
        data_loads.append(load)

    barrier = pltpu.get_barrier_semaphore()

    def greet_group(o, carry):
        pl.semaphore_signal(
            barrier, inc=1, device_id=member(ahead(mine, o, group)), device_id_type=MESH
        )
        return carry

    def greet_z(o, carry):
        pl.semaphore_signal(
            barrier, inc=1, device_id=at(x, ahead(z, o, nz), c, y), device_id_type=MESH
        )
        return carry

    lax.fori_loop(1, group, greet_group, 0, unroll=True)
    lax.fori_loop(1, nz, greet_z, 0, unroll=True)
    sketch_load.wait()

    copies_a = []
    for i, o in enumerate(y_order):
        data_loads[i].wait()
        block = jnp.dot(
            data[rows_of(ahead(y, o, ny)), :], sketch[...], preferred_element_type=F32
        )
        if o == 0:
            own_a[...] = block
        else:
            send_a[o - 1] = block.astype(BF16)
            if i == 0:
                pl.semaphore_wait(barrier, group - 1 + nz - 1)
            copy = remote(
                send_a.at[o - 1],
                recv_a.at[o - 1],
                sem_a.at[0, o - 1],
                sem_a.at[1, o - 1],
                at(x, z, c, ahead(y, o, ny)),
            )
            copy.start()
            copies_a.append(copy)
    first = own_a[...]
    for copy in copies_a:
        copy.wait_recv()
    for o in range(1, ny):
        first = first + recv_a[o - 1].astype(F32)
    mine_t = first.astype(BF16).T
    first_t[y] = mine_t
    copies_f = {}
    for o in y_order[:-1]:
        copy = remote(
            first_t.at[y],
            first_t.at[y],
            sem_f.at[0, o - 1],
            sem_f.at[1, o - 1],
            at(x, z, c, ahead(y, o, ny)),
        )
        copy.start()
        copies_f[o] = copy

    def wait_all(ref, sem):
        pltpu.make_async_copy(ref, ref, sem).wait()

    def gram_scatter(n):
        def step(o, carry):
            to = ahead(mine, o, group)
            remote(
                gsum.at[n, to],
                parts.at[n, o - 1],
                sem_g.at[n, 0, 0],
                sem_g.at[n, 0, 1],
                member(to),
            ).start()
            return carry

        lax.fori_loop(1, group, step, 0, unroll=True)

    def gram_across(n):
        others = parts.at[n, 0 : group - 1]
        wait_all(others, sem_g.at[n, 0, 1])
        zparts[n, 0] = gsum[n, mine] + jnp.sum(others[...], axis=0)

        def send(o, carry):
            remote(
                zparts.at[n, 0],
                zparts.at[n, o],
                sem_g.at[n, 1, 0],
                sem_g.at[n, 1, 1],
                at(x, ahead(z, o, nz), c, y),
            ).start()
            return carry

        lax.fori_loop(1, nz, send, 0, unroll=True)

    def gram_gather(n):
        wait_all(zparts.at[n, 1:nz], sem_g.at[n, 1, 1])

        def add(plane, sums):
            return sums + zparts[n, lax.rem(z - plane + nz, nz)]

        sums = lax.fori_loop(0, nz, add, jnp.zeros((share, K), F32), unroll=True)
        gathered[n, mine] = sums * (1.0 / total)

        def send(o, carry):
            remote(
                gathered.at[n, mine],
                gathered.at[n, mine],
                sem_g.at[n, 2, 0],
                sem_g.at[n, 2, 1],
                member(ahead(mine, o, group)),
            ).start()
            return carry

        lax.fori_loop(1, group, send, 0, unroll=True)

    def gram_done(n):
        wait_all(gathered.at[n, 0 : group - 1], sem_g.at[n, 2, 1])
        return gathered[n].reshape(K, K)

    def gram_sent(n):
        wait_all(parts.at[n, 0 : group - 1], sem_g.at[n, 0, 0])
        wait_all(zparts.at[n, 1:nz], sem_g.at[n, 1, 0])
        wait_all(gathered.at[n, 0 : group - 1], sem_g.at[n, 2, 0])

    gsum[0] = lax.dot_general(mine_t, mine_t, NT, preferred_element_type=F32).reshape(
        group, share, K
    )
    gram_scatter(0)

    def add_rows(offsets, i):
        xd = ahead(x, x_order[i], nx)

        def tile(t, carry):
            cols = pl.ds(pl.multiple_of(xd * quarter + t * ROWS, ROWS), ROWS)
            here = pl.ds(pl.multiple_of(t * ROWS, ROWS), ROWS)
            block = jnp.zeros((K, ROWS), F32)
            for o in offsets:
                block_at = lax.rem(y - o + ny, ny)
                block += jnp.dot(
                    first_t[block_at], data[rows_of(block_at), cols], preferred_element_type=F32
                )
            block = block.reshape(nc, half, ROWS)
            if 0 in offsets:
                own_c[i, :, :, here] = block
            else:
                own_c[i, :, :, here] += block
            return carry

        lax.fori_loop(0, quarter // ROWS, tile, 0)

    for i in range(nx):
        add_rows([0], i)
    for copy in copies_f.values():
        copy.wait_recv()
    gram_across(0)
    copies_c, copies_x = [], []
    for i in range(nx):
        add_rows(range(1, ny), i)
        copy = remote(
            own_c.at[i, 1 - c],
            recv_c.at[i],
            sem_c.at[0, i],
            sem_c.at[1, i],
            at(x, z, 1 - c, y),
        )
        copy.start()
        copies_c.append(copy)
    gram_gather(0)
    for i in range(nx - 1):
        copies_c[i].wait_recv()
        send_x[i] = (own_c[i, c] + recv_c[i]).astype(BF16)
        copy = remote(
            send_x.at[i],
            recv_x.at[i],
            sem_x.at[0, i],
            sem_x.at[1, i],
            at(ahead(x, x_order[i], nx), z, c, y),
        )
        copy.start()
        copies_x.append(copy)

    identity_beside(work, gram_done(0))
    factorise(work, PANELS[:2])

    last = nx - 1
    copies_c[last].wait_recv()
    for copy in copies_x:
        copy.wait_recv()
    copies_z = []
    for o in z_order:
        zd = ahead(z, o, nz)
        cols = pl.ds(pl.multiple_of(zd * LANES, LANES), LANES)
        block = own_c[last, c, :, cols] + recv_c[last, :, cols]
        for j in range(nx - 1):
            block = block + recv_x[j, :, cols].astype(F32)
        if o == 0:
            own_z[...] = block
        else:
            send_z[o - 1] = block.astype(BF16)
            copy = remote(
                send_z.at[o - 1],
                recv_z.at[o - 1],
                sem_z.at[0, o - 1],
                sem_z.at[1, o - 1],
                at(x, zd, c, y),
            )
            copy.start()
            copies_z.append(copy)
    factorise(work, PANELS[2:])
    block = own_z[...]
    for copy in copies_z:
        copy.wait_recv()
    for j in range(nz - 1):
        block = block + recv_z[j].astype(F32)
    pair[c] = block
    copy_p = remote(pair.at[c], pair.at[c], sem_p.at[0], sem_p.at[1], at(x, z, 1 - c, y))
    copy_p.start()
    copy_p.wait_recv()

    own_rows = pl.ds(pl.multiple_of(c * half, half), half)
    solved = dot_split(work[own_rows, K:], pair[...].reshape(K, LANES), NN)

    def cell(px, pz, pc):
        cols = pl.ds(pl.multiple_of((px * nz + pz) * LANES, LANES), LANES)
        return loads.at[pl.ds(pl.multiple_of(pc * half, half), half), cols]

    cell(x, z, c)[...] = (solved * (1.0 / total)).astype(BF16)

    def over_z(o):
        return remote(
            cell(x, z, c),
            cell(x, z, c),
            sem_lz.at[0, o],
            sem_lz.at[1, o],
            at(x, ahead(z, o, nz), c, y),
        )

    def over_x(ox, oz, hops):
        this = cell(lax.rem(x - ox + hops + nx, nx), lax.rem(z - oz + nz, nz), c)
        return remote(
            this,
            this,
            sem_lx.at[0, ox, oz],
            sem_lx.at[1, ox, oz],
            at(lax.rem(x + hops + nx, nx), z, c, y),
        )

    def over_c(ox):
        cols = pl.ds(pl.multiple_of(lax.rem(x - ox + nx, nx) * quarter, quarter), quarter)
        this = loads.at[own_rows, cols]
        return remote(this, this, sem_lc.at[0, ox], sem_lc.at[1, ox], at(x, z, 1 - c, y))

    for o in z_order[:-1]:
        over_z(o).start()
    steps = list(near_first)
    copies_lx = []

    def start_x(ox, oz, hops):
        copy = over_x(ox, oz, hops)
        copy.start()
        copies_lx.append(copy)

    relayed = nz - 3
    for n in range(nz + 2):
        if n < nz:
            oz = steps[n]
            if oz > 0:
                over_z(oz).wait_recv()
            start_x(1, oz, 1)
            if nx > 2:
                start_x(nx - 1, oz, -1)
            if nx == 4 and n >= relayed:
                start_x(2, oz, 2)
            if n == nz - 1:
                over_c(0).start()
        if n >= 2:
            oz = steps[n - 2]
            over_x(1, oz, 1).wait_recv()
            if nx == 4 and n - 2 < relayed and n % 2 == 0:
                start_x(2, oz, 1)
            if nx == 4:
                over_x(3, oz, -1).wait_recv()
                if n - 2 < relayed and n % 2 == 1:
                    start_x(2, oz, -1)

    over_c(1).start()
    if nx == 4:
        over_c(3).start()

    def add_pixels(ox):
        over_c(ox).wait_recv()
        cols = pl.ds(
            pl.multiple_of(lax.rem(x - ox + nx, nx) * quarter, quarter), quarter
        )
        copies = []
        for o in y_order:
            rows = rows_of(ahead(y, o, ny))
            term = lax.dot_general(data[rows, cols], loads[:, cols], NT, preferred_element_type=F32)
            if ox > 0:
                term = acc[o] + term
            if ox != nx // 2 or 2 * o != ny:
                acc[o] = term
            if ox == nx // 2 and o > 0:
                if 2 * o == ny:
                    send_far[...] = term.astype(BF16)
                copy = remote(
                    send_far if 2 * o == ny else acc.at[o],
                    recv_far if 2 * o == ny else recv_d.at[o - 1],
                    sem_d.at[0, o - 1],
                    sem_d.at[1, o - 1],
                    at(x, z, c, ahead(y, o, ny)),
                )
                copy.start()
                copies.append(copy)
        return copies

    add_pixels(0)
    if nx == 4:
        for n, oz in enumerate(steps):
            over_x(2, oz, 1 if n % 2 == 0 else -1).wait_recv()
        over_c(2).start()
        add_pixels(1)
        add_pixels(3)
    copies_d = add_pixels(nx // 2)
    mine_s = acc[0]
    for copy in copies_d:
        copy.wait_recv()
    for o in range(1, ny):
        mine_s = mine_s + (recv_far[...].astype(F32) if 2 * o == ny else recv_d[o - 1])
    second_out[y] = mine_s

    gsum[1] = lax.dot_general(
        mine_s, mine_s, TN, precision=HIGHEST, preferred_element_type=F32
    ).reshape(group, share, K)
    gram_scatter(1)
    gram_across(1)
    gram_gather(1)
    copies_s = []
    for o in y_order[:-1]:
        copy = remote(
            second_out.at[y],
            second_out.at[y],
            sem_s.at[0, o - 1],
            sem_s.at[1, o - 1],
            at(x, z, c, ahead(y, o, ny)),
        )
        copy.start()
        copies_s.append(copy)

    copies = copies_a + list(copies_f.values()) + copies_c + copies_x + copies_z + copies_d
    for copy in copies + copies_lx + [copy_p]:
        copy.wait_send()
    for oz in range(1, nz):
        over_z(oz).wait_send()
    for ox in range(nx):
        over_c(ox).wait_send()
    gram_sent(0)

    identity_beside(work_out, gram_done(1))
    factorise(work_out, PANELS)
    gram_sent(1)
    for copy in copies_s:
        copy.wait()


def basis_kernel(second, work, basis, factor):
    for q in range(second.shape[0]):
        basis[q * ROWS : (q + 1) * ROWS, :] = dot_split(second[q], work[:, K:], NT)
    factor[...] = work[:, :K]


def per_device(dims, data, sketch_matrix):
    nx, nz, nc, ny = dims
    rows, pixels = data.shape
    total = rows * nx * nz * nc
    half, quarter, group = K // nc, nz * LANES, nx * ny * nc
    share = K // group
    assert rows == ny * ROWS and pixels == nx * quarter
    vm = pltpu.VMEM
    dma = pltpu.SemaphoreType.DMA
    second, work = pl.pallas_call(
        functools.partial(sketch_kernel, dims, total),
        out_shape=(
            jax.ShapeDtypeStruct((ny, ROWS, K), F32),
            jax.ShapeDtypeStruct((K, 2 * K), F32),
        ),
        in_specs=[pl.BlockSpec(memory_space=pl.ANY)] * 2,
        out_specs=(pl.BlockSpec(memory_space=pltpu.VMEM),) * 2,
        scratch_shapes=[
            vm((rows, pixels), BF16),
            vm((pixels, K), BF16),
            vm((ny - 1, ROWS, K), BF16),
            vm((ny - 1, ROWS, K), BF16),
            vm((ROWS, K), F32),
            vm((ny, K, ROWS), BF16),
            vm((nx, half, quarter), F32),
            vm((nx, nc, half, quarter), F32),
            vm((nx - 1, half, quarter), BF16),
            vm((nx - 1, half, quarter), BF16),
            vm((nz - 1, half, LANES), BF16),
            vm((nz - 1, half, LANES), BF16),
            vm((half, LANES), F32),
            vm((nc, half, LANES), F32),
            vm((K, pixels), BF16),
            vm((ny, ROWS, K), F32),
            vm((ny - 1, ROWS, K), F32),
            vm((ROWS, K), BF16),
            vm((ROWS, K), BF16),
            vm((2, group, share, K), F32),
            vm((2, group, share, K), F32),
            vm((2, group, share, K), F32),
            vm((2, nz, share, K), F32),
            vm((K, 2 * K), F32),
            dma((ny + 1,)),
            dma((2, ny - 1)),
            dma((2, ny - 1)),
            dma((2, nx)),
            dma((2, nx - 1)),
            dma((2, nz - 1)),
            dma((2,)),
            dma((2, nz)),
            dma((2, nx, nz)),
            dma((2, nx)),
            dma((2, ny - 1)),
            dma((2, ny - 1)),
            dma((2, 3, 2)),
        ],
        compiler_params=pltpu.CompilerParams(
            collective_id=0, has_side_effects=True, vmem_limit_bytes=60 * 1024 * 1024
        ),
        cost_estimate=pl.CostEstimate(
            flops=6 * rows * pixels * K, bytes_accessed=2 * rows * pixels, transcendentals=0
        ),
        name="sketch",
    )(data, sketch_matrix)
    return pl.pallas_call(
        basis_kernel,
        grid=(2,),
        out_shape=(
            jax.ShapeDtypeStruct((rows, K), F32),
            jax.ShapeDtypeStruct((K, K), F32),
        ),
        in_specs=[
            pl.BlockSpec((ny // 2, ROWS, K), lambda q: (q, 0, 0)),
            pl.BlockSpec((K, 2 * K), lambda q: (0, 0)),
        ],
        out_specs=(
            pl.BlockSpec((rows // 2, K), lambda q: (q, 0)),
            pl.BlockSpec((K, K), lambda q: (0, 0)),
        ),
        compiler_params=pltpu.CompilerParams(vmem_limit_bytes=60 * 1024 * 1024),
        name="basis",
    )(second, work)


def solution(mesh):
    in_specs = (P("pos", "pix"), P("pix", None))
    out_specs = (P("pos", None), P())
    return jax.shard_map(
        functools.partial(per_device, dims_of(mesh)),
        mesh=mesh,
        in_specs=in_specs,
        out_specs=out_specs,
        check_vma=False,
    )
```

```python
import functools

import jax
import jax.numpy as jnp
from jax import lax
from jax.experimental import pallas as pl
from jax.experimental.pallas import tpu as pltpu
from jax.sharding import PartitionSpec as P

MESH = pl.DeviceIdType.MESH
F32 = jnp.float32
BF16 = jnp.bfloat16
HIGHEST = lax.Precision.HIGHEST
K = 256
ROWS = 256
LANES = 128
PANEL = 64
PANELS = range(K // PANEL)
SUB = 8

NN = (((1,), (0,)), ((), ()))
NT = (((1,), (1,)), ((), ()))
TN = (((0,), (0,)), ((), ()))


def dims_of(mesh):
    pos, pix = mesh.shape["pos"], mesh.shape["pix"]
    nx = 4 if pos >= 16 else 2
    return nx, pos // (2 * nx), 2, pix


def spread(column):
    return jnp.broadcast_to(column, (SUB, 2 * PANEL))


def factor_panel(square):
    n = square.shape[0]
    at_row = lax.broadcasted_iota(jnp.int32, (n, n), 0)
    at_col = lax.broadcasted_iota(jnp.int32, (n, n), 1)
    eye = jnp.where(at_row == at_col, 1.0, 0.0).astype(F32)
    state = jnp.concatenate([square, eye], axis=1)
    groups = n // SUB
    rows = [state[SUB * g : SUB * (g + 1), :] for g in range(groups)]
    sub = lax.broadcasted_iota(jnp.int32, (SUB, 2 * n), 0)
    lane = lax.broadcasted_iota(jnp.int32, (SUB, 2 * n), 1)
    done = []
    for g in range(groups):
        at = SUB * g
        cols = {
            h: [spread(rows[h][:, at + k : at + k + 1]) for k in range(SUB)]
            for h in range(g, groups)
        }
        top, panel = rows[g], cols[g]
        pivots = jnp.ones((SUB, 2 * n), F32)
        for j in range(SUB):
            pivot = panel[j][j : j + 1, :]
            inverse = 1.0 / pivot
            pivots = jnp.where(sub == j, pivot, pivots)
            heads = [panel[k][j : j + 1, :] for k in range(SUB)]
            row = top[j : j + 1, :]
            under = jnp.where(sub > j, panel[j], 0.0)
            below = under * inverse
            for k in range(j + 1, SUB):
                term = (under * heads[k]) * inverse if k == j + 1 else below * heads[k]
                panel[k] = panel[k] - term
            top = top - below * row
            for h in range(g + 1, groups):
                scaled = cols[h][j] * inverse
                for k in range(j + 1, SUB):
                    cols[h][k] = cols[h][k] - scaled * heads[k]
                rows[h] = rows[h] - scaled * row
        done.append(jnp.where(lane >= sub + at, top * lax.rsqrt(pivots), 0.0))
    state = jnp.concatenate(done, axis=0)
    return state[:, :n], state[:, n:]


def split(value):
    high = value.astype(BF16)
    return high, (value - high.astype(F32)).astype(BF16)


def dot_split(a, b, numbers):
    a_high, a_low = split(a)
    b_high, b_low = split(b)
    dot = functools.partial(
        lax.dot_general, dimension_numbers=numbers, preferred_element_type=F32
    )
    return dot(a_high, b_high) + (dot(a_high, b_low) + dot(a_low, b_high))


def factorise(work, panels, size=K):
    square = None
    for b in panels:
        lo, hi = b * PANEL, (b + 1) * PANEL
        if square is None:
            square = work[lo:hi, lo:hi]
        upper, inverse = factor_panel(square)
        left, right = lo // LANES * LANES, size + -(-hi // LANES) * LANES
        top = jnp.dot(
            inverse, work[lo:hi, left:right], precision=HIGHEST, preferred_element_type=F32
        )
        at_row = lax.broadcasted_iota(jnp.int32, top.shape, 0) + lo
        at_col = lax.broadcasted_iota(jnp.int32, top.shape, 1) + left
        top = jnp.where(at_col >= at_row, top, 0.0)
        if hi < size:
            ahead = top[:, hi - left : hi + PANEL - left]
            square = work[hi : hi + PANEL, hi : hi + PANEL] - lax.dot_general(
                ahead, ahead, TN, precision=HIGHEST, preferred_element_type=F32
            )
            work[hi:, left:right] -= lax.dot_general(
                top[:, hi - left : size - left],
                top,
                TN,
                precision=HIGHEST,
                preferred_element_type=F32,
            )
        if left > 0:
            work[lo:hi, :left] = jnp.zeros((PANEL, left), F32)
        work[lo:hi, left:right] = top
        if right < 2 * size:
            work[lo:hi, right:] = jnp.zeros((PANEL, 2 * size - right), F32)


def identity_beside(work, gram, size=K):
    at_row = lax.broadcasted_iota(jnp.int32, (size, size), 0)
    at_col = lax.broadcasted_iota(jnp.int32, (size, size), 1)
    work[:, :size] = gram
    work[:, size:] = jnp.where(at_row == at_col, 1.0, 0.0).astype(F32)


def sketch_kernel(
    dims,
    total,
    data_hbm,
    sketch_hbm,
    second_out,
    work_out,
    data,
    sketch,
    send_a,
    recv_a,
    own_a,
    first_t,
    recv_c,
    own_c,
    send_x,
    recv_x,
    send_z,
    recv_z,
    own_z,
    pair,
    loads,
    acc,
    recv_d,
    send_far,
    recv_far,
    parts,
    gsum,
    gathered,
    zparts,
    work,
    load_sem,
    sem_a,
    sem_f,
    sem_c,
    sem_x,
    sem_z,
    sem_p,
    sem_lz,
    sem_lx,
    sem_lc,
    sem_d,
    sem_s,
    sem_g,
):
    nx, nz, nc, ny = dims
    half = K // nc
    quarter = nz * LANES
    pos, y = lax.axis_index("pos"), lax.axis_index("pix")
    x, z, c = pos // (nz * nc), lax.rem(pos // nc, nz), lax.rem(pos, nc)
    group = nx * ny * nc
    mine = (x * ny + y) * nc + c
    share = K // group

    def at(px, pz, pc, py):
        return ((px * nz + pz) * nc + pc, py)

    def ahead(i, o, n):
        return lax.rem(i + o, n)

    def member(i):
        return at(i // (ny * nc), z, lax.rem(i, nc), lax.rem(i // nc, ny))

    def remote(src, dst, send_sem, recv_sem, device):
        return pltpu.make_async_remote_copy(
            src_ref=src,
            dst_ref=dst,
            send_sem=send_sem,
            recv_sem=recv_sem,
            device_id=device,
            device_id_type=MESH,
        )

    def rows_of(i):
        return pl.ds(pl.multiple_of(i * ROWS, ROWS), ROWS)

    def by_distance(n):
        return sorted(range(1, n), key=lambda o: (-min(o, n - o), o)) + [0]

    y_order, x_order, z_order = by_distance(ny), by_distance(nx), by_distance(nz)
    near_first = z_order[::-1]

    sketch_load = pltpu.make_async_copy(sketch_hbm, sketch, load_sem.at[ny])
    sketch_load.start()
    data_loads = []
    for o in y_order:
        rows = rows_of(ahead(y, o, ny))
        load = pltpu.make_async_copy(data_hbm.at[rows], data.at[rows], load_sem.at[o])
        load.start()
        data_loads.append(load)

    barrier = pltpu.get_barrier_semaphore()

    def greet_group(o, carry):
        pl.semaphore_signal(
            barrier, inc=1, device_id=member(ahead(mine, o, group)), device_id_type=MESH
        )
        return carry

    def greet_z(o, carry):
        pl.semaphore_signal(
            barrier, inc=1, device_id=at(x, ahead(z, o, nz), c, y), device_id_type=MESH
        )
        return carry

    lax.fori_loop(1, group, greet_group, 0, unroll=True)
    lax.fori_loop(1, nz, greet_z, 0, unroll=True)
    sketch_load.wait()

    copies_a = []
    for i, o in enumerate(y_order):
        data_loads[i].wait()
        block = jnp.dot(
            data[rows_of(ahead(y, o, ny)), :], sketch[...], preferred_element_type=F32
        )
        if o == 0:
            own_a[...] = block
        else:
            send_a[o - 1] = block.astype(BF16)
            if i == 0:
                pl.semaphore_wait(barrier, group - 1 + nz - 1)
            copy = remote(
                send_a.at[o - 1],
                recv_a.at[o - 1],
                sem_a.at[0, o - 1],
                sem_a.at[1, o - 1],
                at(x, z, c, ahead(y, o, ny)),
            )
            copy.start()
            copies_a.append(copy)
    first = own_a[...]
    for copy in copies_a:
        copy.wait_recv()
    for o in range(1, ny):
        first = first + recv_a[o - 1].astype(F32)
    mine_t = first.astype(BF16).T
    first_t[y] = mine_t
    copies_f = {}
    for o in y_order[:-1]:
        copy = remote(
            first_t.at[y],
            first_t.at[y],
            sem_f.at[0, o - 1],
            sem_f.at[1, o - 1],
            at(x, z, c, ahead(y, o, ny)),
        )
        copy.start()
        copies_f[o] = copy

    def wait_all(ref, sem):
        pltpu.make_async_copy(ref, ref, sem).wait()

    def gram_scatter(n):
        def step(o, carry):
            to = ahead(mine, o, group)
            remote(
                gsum.at[n, to],
                parts.at[n, o - 1],
                sem_g.at[n, 0, 0],
                sem_g.at[n, 0, 1],
                member(to),
            ).start()
            return carry

        lax.fori_loop(1, group, step, 0, unroll=True)

    def gram_across(n):
        others = parts.at[n, 0 : group - 1]
        wait_all(others, sem_g.at[n, 0, 1])
        zparts[n, 0] = gsum[n, mine] + jnp.sum(others[...], axis=0)

        def send(o, carry):
            remote(
                zparts.at[n, 0],
                zparts.at[n, o],
                sem_g.at[n, 1, 0],
                sem_g.at[n, 1, 1],
                at(x, ahead(z, o, nz), c, y),
            ).start()
            return carry

        lax.fori_loop(1, nz, send, 0, unroll=True)

    def gram_gather(n):
        wait_all(zparts.at[n, 1:nz], sem_g.at[n, 1, 1])

        def add(plane, sums):
            return sums + zparts[n, lax.rem(z - plane + nz, nz)]

        sums = lax.fori_loop(0, nz, add, jnp.zeros((share, K), F32), unroll=True)
        gathered[n, mine] = sums * (1.0 / total)

        def send(o, carry):
            remote(
                gathered.at[n, mine],
                gathered.at[n, mine],
                sem_g.at[n, 2, 0],
                sem_g.at[n, 2, 1],
                member(ahead(mine, o, group)),
            ).start()
            return carry

        lax.fori_loop(1, group, send, 0, unroll=True)

    def gram_done(n):
        wait_all(gathered.at[n, 0 : group - 1], sem_g.at[n, 2, 1])
        return gathered[n].reshape(K, K)

    def gram_sent(n):
        wait_all(parts.at[n, 0 : group - 1], sem_g.at[n, 0, 0])
        wait_all(zparts.at[n, 1:nz], sem_g.at[n, 1, 0])
        wait_all(gathered.at[n, 0 : group - 1], sem_g.at[n, 2, 0])

    gsum[0] = lax.dot_general(mine_t, mine_t, NT, preferred_element_type=F32).reshape(
        group, share, K
    )
    gram_scatter(0)

    def add_rows(offsets, i):
        xd = ahead(x, x_order[i], nx)

        def tile(t, carry):
            cols = pl.ds(pl.multiple_of(xd * quarter + t * ROWS, ROWS), ROWS)
            here = pl.ds(pl.multiple_of(t * ROWS, ROWS), ROWS)
            block = jnp.zeros((K, ROWS), F32)
            for o in offsets:
                block_at = lax.rem(y - o + ny, ny)
                block += jnp.dot(
                    first_t[block_at], data[rows_of(block_at), cols], preferred_element_type=F32
                )
            block = block.reshape(nc, half, ROWS)
            if 0 in offsets:
                own_c[i, :, :, here] = block
            else:
                own_c[i, :, :, here] += block
            return carry

        lax.fori_loop(0, quarter // ROWS, tile, 0)

    for i in range(nx):
        add_rows([0], i)
    for copy in copies_f.values():
        copy.wait_recv()
    gram_across(0)
    copies_c, copies_x = [], []
    for i in range(nx):
        add_rows(range(1, ny), i)
        copy = remote(
            own_c.at[i, 1 - c],
            recv_c.at[i],
            sem_c.at[0, i],
            sem_c.at[1, i],
            at(x, z, 1 - c, y),
        )
        copy.start()
        copies_c.append(copy)
    gram_gather(0)
    for i in range(nx - 1):
        copies_c[i].wait_recv()
        send_x[i] = (own_c[i, c] + recv_c[i]).astype(BF16)
        copy = remote(
            send_x.at[i],
            recv_x.at[i],
            sem_x.at[0, i],
            sem_x.at[1, i],
            at(ahead(x, x_order[i], nx), z, c, y),
        )
        copy.start()
        copies_x.append(copy)

    identity_beside(work, gram_done(0))
    factorise(work, PANELS[:1])

    last = nx - 1
    copies_c[last].wait_recv()
    for copy in copies_x:
        copy.wait_recv()
    copies_z = []
    for o in z_order:
        zd = ahead(z, o, nz)
        cols = pl.ds(pl.multiple_of(zd * LANES, LANES), LANES)
        block = own_c[last, c, :, cols] + recv_c[last, :, cols]
        for j in range(nx - 1):
            block = block + recv_x[j, :, cols].astype(F32)
        if o == 0:
            own_z[...] = block
        else:
            send_z[o - 1] = block.astype(BF16)
            copy = remote(
                send_z.at[o - 1],
                recv_z.at[o - 1],
                sem_z.at[0, o - 1],
                sem_z.at[1, o - 1],
                at(x, zd, c, y),
            )
            copy.start()
            copies_z.append(copy)
    factorise(work, PANELS[1:])
    block = own_z[...]
    for copy in copies_z:
        copy.wait_recv()
    for j in range(nz - 1):
        block = block + recv_z[j].astype(F32)
    pair[c] = block
    copy_p = remote(pair.at[c], pair.at[c], sem_p.at[0], sem_p.at[1], at(x, z, 1 - c, y))
    copy_p.start()
    copy_p.wait_recv()

    own_rows = pl.ds(pl.multiple_of(c * half, half), half)
    solved = dot_split(work[own_rows, K:], pair[...].reshape(K, LANES), NN)

    def cell(px, pz, pc):
        cols = pl.ds(pl.multiple_of((px * nz + pz) * LANES, LANES), LANES)
        return loads.at[pl.ds(pl.multiple_of(pc * half, half), half), cols]

    cell(x, z, c)[...] = (solved * (1.0 / total)).astype(BF16)

    def over_z(o):
        return remote(
            cell(x, z, c),
            cell(x, z, c),
            sem_lz.at[0, o],
            sem_lz.at[1, o],
            at(x, ahead(z, o, nz), c, y),
        )

    def over_x(ox, oz, hops):
        this = cell(lax.rem(x - ox + hops + nx, nx), lax.rem(z - oz + nz, nz), c)
        return remote(
            this,
            this,
            sem_lx.at[0, ox, oz],
            sem_lx.at[1, ox, oz],
            at(lax.rem(x + hops + nx, nx), z, c, y),
        )

    def over_c(ox):
        cols = pl.ds(pl.multiple_of(lax.rem(x - ox + nx, nx) * quarter, quarter), quarter)
        this = loads.at[own_rows, cols]
        return remote(this, this, sem_lc.at[0, ox], sem_lc.at[1, ox], at(x, z, 1 - c, y))

    for o in z_order[:-1]:
        over_z(o).start()
    steps = list(near_first)
    copies_lx = []

    def start_x(ox, oz, hops):
        copy = over_x(ox, oz, hops)
        copy.start()
        copies_lx.append(copy)

    relayed = nz - 3
    for n in range(nz + 2):
        if n < nz:
            oz = steps[n]
            if oz > 0:
                over_z(oz).wait_recv()
            start_x(1, oz, 1)
            if nx > 2:
                start_x(nx - 1, oz, -1)
            if nx == 4 and n >= relayed:
                start_x(2, oz, 2)
            if n == nz - 1:
                over_c(0).start()
        if n >= 2:
            oz = steps[n - 2]
            over_x(1, oz, 1).wait_recv()
            if nx == 4 and n - 2 < relayed and n % 2 == 0:
                start_x(2, oz, 1)
            if nx == 4:
                over_x(3, oz, -1).wait_recv()
                if n - 2 < relayed and n % 2 == 1:
                    start_x(2, oz, -1)

    over_c(1).start()
    if nx == 4:
        over_c(3).start()

    def add_pixels(ox):
        over_c(ox).wait_recv()
        cols = pl.ds(
            pl.multiple_of(lax.rem(x - ox + nx, nx) * quarter, quarter), quarter
        )
        copies = []
        for o in y_order:
            rows = rows_of(ahead(y, o, ny))
            term = lax.dot_general(data[rows, cols], loads[:, cols], NT, preferred_element_type=F32)
            if ox > 0:
                term = acc[o] + term
            if ox != nx // 2 or 2 * o != ny:
                acc[o] = term
            if ox == nx // 2 and o > 0:
                if 2 * o == ny:
                    send_far[...] = term.astype(BF16)
                copy = remote(
                    send_far if 2 * o == ny else acc.at[o],
                    recv_far if 2 * o == ny else recv_d.at[o - 1],
                    sem_d.at[0, o - 1],
                    sem_d.at[1, o - 1],
                    at(x, z, c, ahead(y, o, ny)),
                )
                copy.start()
                copies.append(copy)
        return copies

    add_pixels(0)
    if nx == 4:
        for n, oz in enumerate(steps):
            over_x(2, oz, 1 if n % 2 == 0 else -1).wait_recv()
        over_c(2).start()
        add_pixels(1)
        add_pixels(3)
    copies_d = add_pixels(nx // 2)
    mine_s = acc[0]
    for copy in copies_d:
        copy.wait_recv()
    for o in range(1, ny):
        mine_s = mine_s + (recv_far[...].astype(F32) if 2 * o == ny else recv_d[o - 1])
    second_out[y] = mine_s

    gsum[1] = lax.dot_general(
        mine_s, mine_s, TN, precision=HIGHEST, preferred_element_type=F32
    ).reshape(group, share, K)
    gram_scatter(1)
    gram_across(1)
    gram_gather(1)
    copies_s = []
    for o in y_order[:-1]:
        copy = remote(
            second_out.at[y],
            second_out.at[y],
            sem_s.at[0, o - 1],
            sem_s.at[1, o - 1],
            at(x, z, c, ahead(y, o, ny)),
        )
        copy.start()
        copies_s.append(copy)

    copies = copies_a + list(copies_f.values()) + copies_c + copies_x + copies_z + copies_d
    for copy in copies + copies_lx + [copy_p]:
        copy.wait_send()
    for oz in range(1, nz):
        over_z(oz).wait_send()
    for ox in range(nx):
        over_c(ox).wait_send()
    gram_sent(0)

    identity_beside(work_out, gram_done(1))
    factorise(work_out, PANELS)
    gram_sent(1)
    for copy in copies_s:
        copy.wait()


def basis_kernel(second, work, basis, factor):
    for q in range(second.shape[0]):
        basis[q * ROWS : (q + 1) * ROWS, :] = dot_split(second[q], work[:, K:], NT)
    factor[...] = work[:, :K]


def per_device(dims, data, sketch_matrix):
    nx, nz, nc, ny = dims
    rows, pixels = data.shape
    total = rows * nx * nz * nc
    half, quarter, group = K // nc, nz * LANES, nx * ny * nc
    share = K // group
    assert rows == ny * ROWS and pixels == nx * quarter
    vm = pltpu.VMEM
    dma = pltpu.SemaphoreType.DMA
    second, work = pl.pallas_call(
        functools.partial(sketch_kernel, dims, total),
        out_shape=(
            jax.ShapeDtypeStruct((ny, ROWS, K), F32),
            jax.ShapeDtypeStruct((K, 2 * K), F32),
        ),
        in_specs=[pl.BlockSpec(memory_space=pl.ANY)] * 2,
        out_specs=(pl.BlockSpec(memory_space=pltpu.VMEM),) * 2,
        scratch_shapes=[
            vm((rows, pixels), BF16),
            vm((pixels, K), BF16),
            vm((ny - 1, ROWS, K), BF16),
            vm((ny - 1, ROWS, K), BF16),
            vm((ROWS, K), F32),
            vm((ny, K, ROWS), BF16),
            vm((nx, half, quarter), F32),
            vm((nx, nc, half, quarter), F32),
            vm((nx - 1, half, quarter), BF16),
            vm((nx - 1, half, quarter), BF16),
            vm((nz - 1, half, LANES), BF16),
            vm((nz - 1, half, LANES), BF16),
            vm((half, LANES), F32),
            vm((nc, half, LANES), F32),
            vm((K, pixels), BF16),
            vm((ny, ROWS, K), F32),
            vm((ny - 1, ROWS, K), F32),
            vm((ROWS, K), BF16),
            vm((ROWS, K), BF16),
            vm((2, group, share, K), F32),
            vm((2, group, share, K), F32),
            vm((2, group, share, K), F32),
            vm((2, nz, share, K), F32),
            vm((K, 2 * K), F32),
            dma((ny + 1,)),
            dma((2, ny - 1)),
            dma((2, ny - 1)),
            dma((2, nx)),
            dma((2, nx - 1)),
            dma((2, nz - 1)),
            dma((2,)),
            dma((2, nz)),
            dma((2, nx, nz)),
            dma((2, nx)),
            dma((2, ny - 1)),
            dma((2, ny - 1)),
            dma((2, 3, 2)),
        ],
        compiler_params=pltpu.CompilerParams(
            collective_id=0, has_side_effects=True, vmem_limit_bytes=60 * 1024 * 1024
        ),
        cost_estimate=pl.CostEstimate(
            flops=6 * rows * pixels * K, bytes_accessed=2 * rows * pixels, transcendentals=0
        ),
        name="sketch",
    )(data, sketch_matrix)
    return pl.pallas_call(
        basis_kernel,
        grid=(2,),
        out_shape=(
            jax.ShapeDtypeStruct((rows, K), F32),
            jax.ShapeDtypeStruct((K, K), F32),
        ),
        in_specs=[
            pl.BlockSpec((ny // 2, ROWS, K), lambda q: (q, 0, 0)),
            pl.BlockSpec((K, 2 * K), lambda q: (0, 0)),
        ],
        out_specs=(
            pl.BlockSpec((rows // 2, K), lambda q: (q, 0)),
            pl.BlockSpec((K, K), lambda q: (0, 0)),
        ),
        compiler_params=pltpu.CompilerParams(vmem_limit_bytes=60 * 1024 * 1024),
        name="basis",
    )(second, work)


def solution(mesh):
    in_specs = (P("pos", "pix"), P("pix", None))
    out_specs = (P("pos", None), P())
    return jax.shard_map(
        functools.partial(per_device, dims_of(mesh)),
        mesh=mesh,
        in_specs=in_specs,
        out_specs=out_specs,
        check_vma=False,
    )
```

```python
import functools

import jax
import jax.numpy as jnp
from jax import lax
from jax.experimental import pallas as pl
from jax.experimental.pallas import tpu as pltpu
from jax.sharding import PartitionSpec as P

MESH = pl.DeviceIdType.MESH
F32 = jnp.float32
BF16 = jnp.bfloat16
HIGHEST = lax.Precision.HIGHEST
K = 256
ROWS = 256
LANES = 128
PANEL = 64
PANELS = range(K // PANEL)
SUB = 8

NN = (((1,), (0,)), ((), ()))
NT = (((1,), (1,)), ((), ()))
TN = (((0,), (0,)), ((), ()))


def dims_of(mesh):
    pos, pix = mesh.shape["pos"], mesh.shape["pix"]
    nx = 4 if pos >= 16 else 2
    return nx, pos // (2 * nx), 2, pix


def spread(column):
    return jnp.broadcast_to(column, (SUB, 2 * PANEL))


def factor_panel(square):
    n = square.shape[0]
    at_row = lax.broadcasted_iota(jnp.int32, (n, n), 0)
    at_col = lax.broadcasted_iota(jnp.int32, (n, n), 1)
    eye = jnp.where(at_row == at_col, 1.0, 0.0).astype(F32)
    state = jnp.concatenate([square, eye], axis=1)
    groups = n // SUB
    rows = [state[SUB * g : SUB * (g + 1), :] for g in range(groups)]
    sub = lax.broadcasted_iota(jnp.int32, (SUB, 2 * n), 0)
    lane = lax.broadcasted_iota(jnp.int32, (SUB, 2 * n), 1)
    done = []
    for g in range(groups):
        at = SUB * g
        cols = {
            h: [spread(rows[h][:, at + k : at + k + 1]) for k in range(SUB)]
            for h in range(g, groups)
        }
        top, panel = rows[g], cols[g]
        pivots = jnp.ones((SUB, 2 * n), F32)
        for j in range(SUB):
            pivot = panel[j][j : j + 1, :]
            inverse = 1.0 / pivot
            pivots = jnp.where(sub == j, pivot, pivots)
            heads = [panel[k][j : j + 1, :] for k in range(SUB)]
            row = top[j : j + 1, :]
            under = jnp.where(sub > j, panel[j], 0.0)
            below = under * inverse
            for k in range(j + 1, SUB):
                term = (under * heads[k]) * inverse if k == j + 1 else below * heads[k]
                panel[k] = panel[k] - term
            top = top - below * row
            for h in range(g + 1, groups):
                scaled = cols[h][j] * inverse
                for k in range(j + 1, SUB):
                    cols[h][k] = cols[h][k] - scaled * heads[k]
                rows[h] = rows[h] - scaled * row
        done.append(jnp.where(lane >= sub + at, top * lax.rsqrt(pivots), 0.0))
    state = jnp.concatenate(done, axis=0)
    return state[:, :n], state[:, n:]


def split(value):
    high = value.astype(BF16)
    return high, (value - high.astype(F32)).astype(BF16)


def dot_split(a, b, numbers):
    a_high, a_low = split(a)
    b_high, b_low = split(b)
    dot = functools.partial(
        lax.dot_general, dimension_numbers=numbers, preferred_element_type=F32
    )
    return dot(a_high, b_high) + (dot(a_high, b_low) + dot(a_low, b_high))


def factorise(work, panels, size=K):
    square = None
    for b in panels:
        lo, hi = b * PANEL, (b + 1) * PANEL
        if square is None:
            square = work[lo:hi, lo:hi]
        upper, inverse = factor_panel(square)
        left, right = lo // LANES * LANES, size + -(-hi // LANES) * LANES
        top = jnp.dot(
            inverse, work[lo:hi, left:right], precision=HIGHEST, preferred_element_type=F32
        )
        at_row = lax.broadcasted_iota(jnp.int32, top.shape, 0) + lo
        at_col = lax.broadcasted_iota(jnp.int32, top.shape, 1) + left
        top = jnp.where(at_col >= at_row, top, 0.0)
        if hi < size:
            ahead = top[:, hi - left : hi + PANEL - left]
            square = work[hi : hi + PANEL, hi : hi + PANEL] - lax.dot_general(
                ahead, ahead, TN, precision=HIGHEST, preferred_element_type=F32
            )
            work[hi:, left:right] -= lax.dot_general(
                top[:, hi - left : size - left],
                top,
                TN,
                precision=HIGHEST,
                preferred_element_type=F32,
            )
        if left > 0:
            work[lo:hi, :left] = jnp.zeros((PANEL, left), F32)
        work[lo:hi, left:right] = top
        if right < 2 * size:
            work[lo:hi, right:] = jnp.zeros((PANEL, 2 * size - right), F32)


def identity_beside(work, gram, size=K):
    at_row = lax.broadcasted_iota(jnp.int32, (size, size), 0)
    at_col = lax.broadcasted_iota(jnp.int32, (size, size), 1)
    work[:, :size] = gram
    work[:, size:] = jnp.where(at_row == at_col, 1.0, 0.0).astype(F32)


def sketch_kernel(
    dims,
    total,
    data_hbm,
    sketch_hbm,
    second_out,
    work_out,
    data,
    sketch,
    send_a,
    recv_a,
    own_a,
    first_t,
    recv_c,
    own_c,
    send_x,
    recv_x,
    send_z,
    recv_z,
    own_z,
    pair,
    loads,
    acc,
    recv_d,
    send_far,
    recv_far,
    parts,
    gsum,
    gathered,
    zparts,
    work,
    load_sem,
    sem_a,
    sem_f,
    sem_c,
    sem_x,
    sem_z,
    sem_p,
    sem_lz,
    sem_lx,
    sem_lc,
    sem_d,
    sem_s,
    sem_g,
):
    nx, nz, nc, ny = dims
    half = K // nc
    quarter = nz * LANES
    pos, y = lax.axis_index("pos"), lax.axis_index("pix")
    x, z, c = pos // (nz * nc), lax.rem(pos // nc, nz), lax.rem(pos, nc)
    group = nx * ny * nc
    mine = (x * ny + y) * nc + c
    share = K // group

    def at(px, pz, pc, py):
        return ((px * nz + pz) * nc + pc, py)

    def ahead(i, o, n):
        return lax.rem(i + o, n)

    def member(i):
        return at(i // (ny * nc), z, lax.rem(i, nc), lax.rem(i // nc, ny))

    def remote(src, dst, send_sem, recv_sem, device):
        return pltpu.make_async_remote_copy(
            src_ref=src,
            dst_ref=dst,
            send_sem=send_sem,
            recv_sem=recv_sem,
            device_id=device,
            device_id_type=MESH,
        )

    def rows_of(i):
        return pl.ds(pl.multiple_of(i * ROWS, ROWS), ROWS)

    def by_distance(n):
        return sorted(range(1, n), key=lambda o: (-min(o, n - o), o)) + [0]

    y_order, x_order, z_order = by_distance(ny), by_distance(nx), by_distance(nz)
    near_first = z_order[::-1]

    sketch_load = pltpu.make_async_copy(sketch_hbm, sketch, load_sem.at[ny])
    sketch_load.start()
    data_loads = []
    for o in y_order:
        rows = rows_of(ahead(y, o, ny))
        load = pltpu.make_async_copy(data_hbm.at[rows], data.at[rows], load_sem.at[o])
        load.start()
        data_loads.append(load)

    barrier = pltpu.get_barrier_semaphore()

    def greet_group(o, carry):
        pl.semaphore_signal(
            barrier, inc=1, device_id=member(ahead(mine, o, group)), device_id_type=MESH
        )
        return carry

    def greet_z(o, carry):
        pl.semaphore_signal(
            barrier, inc=1, device_id=at(x, ahead(z, o, nz), c, y), device_id_type=MESH
        )
        return carry

    lax.fori_loop(1, group, greet_group, 0, unroll=True)
    lax.fori_loop(1, nz, greet_z, 0, unroll=True)
    sketch_load.wait()

    copies_a = []
    for i, o in enumerate(y_order):
        data_loads[i].wait()
        block = jnp.dot(
            data[rows_of(ahead(y, o, ny)), :], sketch[...], preferred_element_type=F32
        )
        if o == 0:
            own_a[...] = block
        else:
            send_a[o - 1] = block.astype(BF16)
            if i == 0:
                pl.semaphore_wait(barrier, group - 1 + nz - 1)
            copy = remote(
                send_a.at[o - 1],
                recv_a.at[o - 1],
                sem_a.at[0, o - 1],
                sem_a.at[1, o - 1],
                at(x, z, c, ahead(y, o, ny)),
            )
            copy.start()
            copies_a.append(copy)
    first = own_a[...]
    for copy in copies_a:
        copy.wait_recv()
    for o in range(1, ny):
        first = first + recv_a[o - 1].astype(F32)
    mine_t = first.astype(BF16).T
    first_t[y] = mine_t
    copies_f = {}
    for o in y_order[:-1]:
        copy = remote(
            first_t.at[y],
            first_t.at[y],
            sem_f.at[0, o - 1],
            sem_f.at[1, o - 1],
            at(x, z, c, ahead(y, o, ny)),
        )
        copy.start()
        copies_f[o] = copy

    def wait_all(ref, sem):
        pltpu.make_async_copy(ref, ref, sem).wait()

    def gram_scatter(n):
        def step(o, carry):
            to = ahead(mine, o, group)
            remote(
                gsum.at[n, to],
                parts.at[n, o - 1],
                sem_g.at[n, 0, 0],
                sem_g.at[n, 0, 1],
                member(to),
            ).start()
            return carry

        lax.fori_loop(1, group, step, 0, unroll=True)

    def gram_across(n):
        others = parts.at[n, 0 : group - 1]
        wait_all(others, sem_g.at[n, 0, 1])
        zparts[n, 0] = gsum[n, mine] + jnp.sum(others[...], axis=0)

        def send(o, carry):
            remote(
                zparts.at[n, 0],
                zparts.at[n, o],
                sem_g.at[n, 1, 0],
                sem_g.at[n, 1, 1],
                at(x, ahead(z, o, nz), c, y),
            ).start()
            return carry

        lax.fori_loop(1, nz, send, 0, unroll=True)

    def gram_gather(n):
        wait_all(zparts.at[n, 1:nz], sem_g.at[n, 1, 1])

        def add(plane, sums):
            return sums + zparts[n, lax.rem(z - plane + nz, nz)]

        sums = lax.fori_loop(0, nz, add, jnp.zeros((share, K), F32), unroll=True)
        gathered[n, mine] = sums * (1.0 / total)

        def send(o, carry):
            remote(
                gathered.at[n, mine],
                gathered.at[n, mine],
                sem_g.at[n, 2, 0],
                sem_g.at[n, 2, 1],
                member(ahead(mine, o, group)),
            ).start()
            return carry

        lax.fori_loop(1, group, send, 0, unroll=True)

    def gram_done(n):
        wait_all(gathered.at[n, 0 : group - 1], sem_g.at[n, 2, 1])
        return gathered[n].reshape(K, K)

    def gram_sent(n):
        wait_all(parts.at[n, 0 : group - 1], sem_g.at[n, 0, 0])
        wait_all(zparts.at[n, 1:nz], sem_g.at[n, 1, 0])
        wait_all(gathered.at[n, 0 : group - 1], sem_g.at[n, 2, 0])

    gsum[0] = lax.dot_general(mine_t, mine_t, NT, preferred_element_type=F32).reshape(
        group, share, K
    )
    gram_scatter(0)

    def add_rows(offsets, i):
        xd = ahead(x, x_order[i], nx)

        def tile(t, carry):
            cols = pl.ds(pl.multiple_of(xd * quarter + t * ROWS, ROWS), ROWS)
            here = pl.ds(pl.multiple_of(t * ROWS, ROWS), ROWS)
            block = jnp.zeros((K, ROWS), F32)
            for o in offsets:
                block_at = lax.rem(y - o + ny, ny)
                block += jnp.dot(
                    first_t[block_at], data[rows_of(block_at), cols], preferred_element_type=F32
                )
            block = block.reshape(nc, half, ROWS)
            if 0 in offsets:
                own_c[i, :, :, here] = block
            else:
                own_c[i, :, :, here] += block
            return carry

        lax.fori_loop(0, quarter // ROWS, tile, 0)

    for i in range(nx):
        add_rows([0], i)
    for copy in copies_f.values():
        copy.wait_recv()
    gram_across(0)
    copies_c, copies_x = [], []

    def send_over_x(i):
        copies_c[i].wait_recv()
        send_x[i] = (own_c[i, c] + recv_c[i]).astype(BF16)
        copy = remote(
            send_x.at[i],
            recv_x.at[i],
            sem_x.at[0, i],
            sem_x.at[1, i],
            at(ahead(x, x_order[i], nx), z, c, y),
        )
        copy.start()
        copies_x.append(copy)

    for i in range(nx):
        add_rows(range(1, ny), i)
        copy = remote(
            own_c.at[i, 1 - c],
            recv_c.at[i],
            sem_c.at[0, i],
            sem_c.at[1, i],
            at(x, z, 1 - c, y),
        )
        copy.start()
        copies_c.append(copy)
        if i == 1:
            send_over_x(0)
    gram_gather(0)
    for i in range(1, nx - 1):
        send_over_x(i)

    identity_beside(work, gram_done(0))
    factorise(work, PANELS[:1])

    last = nx - 1
    copies_c[last].wait_recv()
    for copy in copies_x:
        copy.wait_recv()
    copies_z = []
    for o in z_order:
        zd = ahead(z, o, nz)
        cols = pl.ds(pl.multiple_of(zd * LANES, LANES), LANES)
        block = own_c[last, c, :, cols] + recv_c[last, :, cols]
        for j in range(nx - 1):
            block = block + recv_x[j, :, cols].astype(F32)
        if o == 0:
            own_z[...] = block
        else:
            send_z[o - 1] = block.astype(BF16)
            copy = remote(
                send_z.at[o - 1],
                recv_z.at[o - 1],
                sem_z.at[0, o - 1],
                sem_z.at[1, o - 1],
                at(x, zd, c, y),
            )
            copy.start()
            copies_z.append(copy)
    factorise(work, PANELS[1:])
    block = own_z[...]
    for copy in copies_z:
        copy.wait_recv()
    for j in range(nz - 1):
        block = block + recv_z[j].astype(F32)
    pair[c] = block
    copy_p = remote(pair.at[c], pair.at[c], sem_p.at[0], sem_p.at[1], at(x, z, 1 - c, y))
    copy_p.start()
    copy_p.wait_recv()

    own_rows = pl.ds(pl.multiple_of(c * half, half), half)
    solved = dot_split(work[own_rows, K:], pair[...].reshape(K, LANES), NN)

    def cell(px, pz, pc):
        cols = pl.ds(pl.multiple_of((px * nz + pz) * LANES, LANES), LANES)
        return loads.at[pl.ds(pl.multiple_of(pc * half, half), half), cols]

    cell(x, z, c)[...] = (solved * (1.0 / total)).astype(BF16)

    def over_z(o):
        return remote(
            cell(x, z, c),
            cell(x, z, c),
            sem_lz.at[0, o],
            sem_lz.at[1, o],
            at(x, ahead(z, o, nz), c, y),
        )

    def over_x(ox, oz, hops):
        this = cell(lax.rem(x - ox + hops + nx, nx), lax.rem(z - oz + nz, nz), c)
        return remote(
            this,
            this,
            sem_lx.at[0, ox, oz],
            sem_lx.at[1, ox, oz],
            at(lax.rem(x + hops + nx, nx), z, c, y),
        )

    def over_c(ox):
        cols = pl.ds(pl.multiple_of(lax.rem(x - ox + nx, nx) * quarter, quarter), quarter)
        this = loads.at[own_rows, cols]
        return remote(this, this, sem_lc.at[0, ox], sem_lc.at[1, ox], at(x, z, 1 - c, y))

    for o in z_order[:-1]:
        over_z(o).start()
    steps = list(near_first)
    copies_lx = []

    def start_x(ox, oz, hops):
        copy = over_x(ox, oz, hops)
        copy.start()
        copies_lx.append(copy)

    relayed = nz - 3
    for n in range(nz + 2):
        if n < nz:
            oz = steps[n]
            if oz > 0:
                over_z(oz).wait_recv()
            start_x(1, oz, 1)
            if nx > 2:
                start_x(nx - 1, oz, -1)
            if nx == 4 and n >= relayed:
                start_x(2, oz, 2)
            if n == nz - 1:
                over_c(0).start()
        if n >= 2:
            oz = steps[n - 2]
            over_x(1, oz, 1).wait_recv()
            if nx == 4 and n - 2 < relayed and n % 2 == 0:
                start_x(2, oz, 1)
            if nx == 4:
                over_x(3, oz, -1).wait_recv()
                if n - 2 < relayed and n % 2 == 1:
                    start_x(2, oz, -1)

    over_c(1).start()
    if nx == 4:
        over_c(3).start()

    def add_pixels(ox):
        over_c(ox).wait_recv()
        cols = pl.ds(
            pl.multiple_of(lax.rem(x - ox + nx, nx) * quarter, quarter), quarter
        )
        copies = []
        for o in y_order:
            rows = rows_of(ahead(y, o, ny))
            term = lax.dot_general(data[rows, cols], loads[:, cols], NT, preferred_element_type=F32)
            if ox > 0:
                term = acc[o] + term
            if ox != nx // 2 or 2 * o != ny:
                acc[o] = term
            if ox == nx // 2 and o > 0:
                if 2 * o == ny:
                    send_far[...] = term.astype(BF16)
                copy = remote(
                    send_far if 2 * o == ny else acc.at[o],
                    recv_far if 2 * o == ny else recv_d.at[o - 1],
                    sem_d.at[0, o - 1],
                    sem_d.at[1, o - 1],
                    at(x, z, c, ahead(y, o, ny)),
                )
                copy.start()
                copies.append(copy)
        return copies

    add_pixels(0)
    if nx == 4:
        for n, oz in enumerate(steps):
            over_x(2, oz, 1 if n % 2 == 0 else -1).wait_recv()
        over_c(2).start()
        add_pixels(1)
        add_pixels(3)
    copies_d = add_pixels(nx // 2)
    mine_s = acc[0]
    for copy in copies_d:
        copy.wait_recv()
    for o in range(1, ny):
        mine_s = mine_s + (recv_far[...].astype(F32) if 2 * o == ny else recv_d[o - 1])
    second_out[y] = mine_s

    gsum[1] = lax.dot_general(
        mine_s, mine_s, TN, precision=HIGHEST, preferred_element_type=F32
    ).reshape(group, share, K)
    gram_scatter(1)
    gram_across(1)
    gram_gather(1)
    copies_s = []
    for o in y_order[:-1]:
        copy = remote(
            second_out.at[y],
            second_out.at[y],
            sem_s.at[0, o - 1],
            sem_s.at[1, o - 1],
            at(x, z, c, ahead(y, o, ny)),
        )
        copy.start()
        copies_s.append(copy)

    copies = copies_a + list(copies_f.values()) + copies_c + copies_x + copies_z + copies_d
    for copy in copies + copies_lx + [copy_p]:
        copy.wait_send()
    for oz in range(1, nz):
        over_z(oz).wait_send()
    for ox in range(nx):
        over_c(ox).wait_send()
    gram_sent(0)

    identity_beside(work_out, gram_done(1))
    factorise(work_out, PANELS)
    gram_sent(1)
    for copy in copies_s:
        copy.wait()


def basis_kernel(second, work, basis, factor):
    for q in range(second.shape[0]):
        basis[q * ROWS : (q + 1) * ROWS, :] = dot_split(second[q], work[:, K:], NT)
    factor[...] = work[:, :K]


def per_device(dims, data, sketch_matrix):
    nx, nz, nc, ny = dims
    rows, pixels = data.shape
    total = rows * nx * nz * nc
    half, quarter, group = K // nc, nz * LANES, nx * ny * nc
    share = K // group
    assert rows == ny * ROWS and pixels == nx * quarter
    vm = pltpu.VMEM
    dma = pltpu.SemaphoreType.DMA
    second, work = pl.pallas_call(
        functools.partial(sketch_kernel, dims, total),
        out_shape=(
            jax.ShapeDtypeStruct((ny, ROWS, K), F32),
            jax.ShapeDtypeStruct((K, 2 * K), F32),
        ),
        in_specs=[pl.BlockSpec(memory_space=pl.ANY)] * 2,
        out_specs=(pl.BlockSpec(memory_space=pltpu.VMEM),) * 2,
        scratch_shapes=[
            vm((rows, pixels), BF16),
            vm((pixels, K), BF16),
            vm((ny - 1, ROWS, K), BF16),
            vm((ny - 1, ROWS, K), BF16),
            vm((ROWS, K), F32),
            vm((ny, K, ROWS), BF16),
            vm((nx, half, quarter), F32),
            vm((nx, nc, half, quarter), F32),
            vm((nx - 1, half, quarter), BF16),
            vm((nx - 1, half, quarter), BF16),
            vm((nz - 1, half, LANES), BF16),
            vm((nz - 1, half, LANES), BF16),
            vm((half, LANES), F32),
            vm((nc, half, LANES), F32),
            vm((K, pixels), BF16),
            vm((ny, ROWS, K), F32),
            vm((ny - 1, ROWS, K), F32),
            vm((ROWS, K), BF16),
            vm((ROWS, K), BF16),
            vm((2, group, share, K), F32),
            vm((2, group, share, K), F32),
            vm((2, group, share, K), F32),
            vm((2, nz, share, K), F32),
            vm((K, 2 * K), F32),
            dma((ny + 1,)),
            dma((2, ny - 1)),
            dma((2, ny - 1)),
            dma((2, nx)),
            dma((2, nx - 1)),
            dma((2, nz - 1)),
            dma((2,)),
            dma((2, nz)),
            dma((2, nx, nz)),
            dma((2, nx)),
            dma((2, ny - 1)),
            dma((2, ny - 1)),
            dma((2, 3, 2)),
        ],
        compiler_params=pltpu.CompilerParams(
            collective_id=0, has_side_effects=True, vmem_limit_bytes=60 * 1024 * 1024
        ),
        cost_estimate=pl.CostEstimate(
            flops=6 * rows * pixels * K, bytes_accessed=2 * rows * pixels, transcendentals=0
        ),
        name="sketch",
    )(data, sketch_matrix)
    return pl.pallas_call(
        basis_kernel,
        grid=(2,),
        out_shape=(
            jax.ShapeDtypeStruct((rows, K), F32),
            jax.ShapeDtypeStruct((K, K), F32),
        ),
        in_specs=[
            pl.BlockSpec((ny // 2, ROWS, K), lambda q: (q, 0, 0)),
            pl.BlockSpec((K, 2 * K), lambda q: (0, 0)),
        ],
        out_specs=(
            pl.BlockSpec((rows // 2, K), lambda q: (q, 0)),
            pl.BlockSpec((K, K), lambda q: (0, 0)),
        ),
        compiler_params=pltpu.CompilerParams(vmem_limit_bytes=60 * 1024 * 1024),
        name="basis",
    )(second, work)


def solution(mesh):
    in_specs = (P("pos", "pix"), P("pix", None))
    out_specs = (P("pos", None), P())
    return jax.shard_map(
        functools.partial(per_device, dims_of(mesh)),
        mesh=mesh,
        in_specs=in_specs,
        out_specs=out_specs,
        check_vma=False,
    )
```
